32 devices in a mesh: groups: 2 (over y), seq: 4 (over z), chan: 2 (over x), sub: 2 (over core).
Axes of the slice: x: 2, y: 2, z: 4, core: 2. Of those that a mesh axis runs over, the one named last changes fastest.
Arguments:
- features: bfloat16 [1024, 96], P(('groups', 'seq'), 'chan'), parts along dimension 0, may hold values from -6 to 6
- proj: bfloat16 [96, 32], P('chan'), may hold values from -0.625 to 0.625
- kernel: float32 [2, 32, 9], P(None, 'chan'), may hold values from -2.4 to 2.4
- mix: bfloat16 [2, 32, 32], P(None, None, 'chan'), may hold values from -1 to 1
- readout: float32 [32], replicated, may hold values from -1 to 1
- dilations: int32 [2], replicated, may hold values from 1 to 8, as said below
- chrom_lengths: int32 [4], replicated, may hold values from 42 to 256, as said below
- pairs: int32 [32, 2], P(('groups', 'seq')), parts along dimension 0, may hold values from 0 to 3, as said below
- contact_cot: float32 [128, 1024], P('sub', ('groups', 'seq')), parts along dimension 1, may hold values from -6 to 6
- trans_cot: float32 [32, 128, 128], P(('groups', 'seq'), ('chan', 'sub')), parts along dimension 0, may hold values from -6 to 6
Outputs:
- contact: float32 [128, 1024], P('sub', ('groups', 'seq')), parts along dimension 1
- trans_maps: float32 [32, 128, 128], P(('groups', 'seq'), ('chan', 'sub')), parts along dimension 0
- grad_features: float32 [1024, 96], P(('groups', 'seq'), 'chan'), parts along dimension 0
- grad_proj: float32 [192, 32], P(('groups', 'chan')), parts along dimension 0
- grad_kernel: float32 [4, 32, 9], P('groups', 'chan'), parts along dimension 0
- grad_mix: float32 [4, 32, 32], P('groups', None, 'chan'), parts along dimension 0
The draws below stay inside these ranges and needn't reach their ends.
There are 2 independent parts, one for each index of `groups`. The reference program is written for one: setup_inputs(seed, part) draws one part's arguments, and reference() takes and returns one part's arrays. A program takes and returns all parts, laid end to end along the dimension named above; an argument that names none is the same for every part. Nothing has to cross between parts.
Inputs may be any that keep to these rules, and one draw needn't show every extreme that they name: `dilations`: at least one layer has dilation 8. `chrom_lengths`: the lengths sum to 512; one is exactly 256 and one is exactly the least. `pairs`: the two blocks of a row differ; each block is the first block of exactly 4 rows.
All inputs are finite; a program needn't handle non-finite values.
Results may differ from the reference program's by a relative error of at most 0.006.
The reference program's roundings to bfloat16 on the way count: a program that leaves them out, or rounds other values in their place, can miss the bound.
Values may be sent and summed in bfloat16 or wider, within the bound.
A program may use at most 64 MiB of HBM per device.

```python
import jax
import jax.numpy as jnp
from jax import lax

C = 32
F = 96
BAND = 128
DMAX = 8
LAYERS = 2
NCHROM = 4
BIN_DEV = 128
BINS = 512
BLOCKS = 4
PAIRS = 16
MOSTLEN = 256


def draw_dilations(key, part):
    key = jax.random.fold_in(key, 7)
    key_value, key_place = jax.random.split(key)
    values = jax.random.randint(key_value, (LAYERS,), 1, DMAX + 1)
    place = jax.random.randint(key_place, (), 0, LAYERS)
    return jnp.where(jnp.arange(LAYERS) == place, DMAX, values).astype(jnp.int32)


def draw_chrom_lengths(key, part):
    key = jax.random.fold_in(key, 5)
    key_cut, key_order = jax.random.split(key)
    remaining = BINS - MOSTLEN
    least = remaining // 6
    spare = remaining - 3 * least
    cut_point = jax.random.randint(key_cut, (), 0, spare + 1)
    pieces = jnp.stack([jnp.int32(MOSTLEN), jnp.int32(least), least + cut_point, least + spare - cut_point])
    order = jax.random.permutation(key_order, NCHROM)
    return pieces[order].astype(jnp.int32)


def draw_pairs(key, part):
    key = jax.random.fold_in(key, 11)
    key_first, key_gap = jax.random.split(key)
    first_block = jax.random.permutation(key_first, PAIRS) % BLOCKS
    block_gap = jax.random.randint(key_gap, (PAIRS,), 1, BLOCKS)
    second_block = (first_block + block_gap) % BLOCKS
    return jnp.stack([first_block, second_block], axis=1).astype(jnp.int32)


def block_levels(rng, dims, cuts, smallest, high):
    gain, own = 1.0, jax.random.fold_in(rng, 6)
    for position, parts in cuts:
        steps = jnp.exp(jax.random.uniform(jax.random.fold_in(own, position), (parts,), jnp.float32, smallest / len(cuts), high / len(cuts)))
        gain = gain * jnp.repeat(steps, dims[position] // parts).reshape([-1 if axis == position else 1 for axis in range(len(dims))])
    return gain


def scatter_about(own_key, shape, spread, bound, cuts=(), kind=jnp.bfloat16):
    array = spread * jax.random.normal(own_key, shape, jnp.float32)
    if cuts:
        array = array * block_levels(own_key, shape, cuts, -0.22, 0.18)
    return jnp.clip(array, -bound, bound).astype(kind)


def setup_inputs(seed: int = 0, part: int = 0) -> dict:
    seeds = jax.random.split(jax.random.key(seed), 11)
    own_keys = jax.random.split(jax.random.fold_in(seeds[10], part), 11)
    features = scatter_about(own_keys[0], (BINS, F), 1.0, 6.0, ((0, 4), (1, 2)))
    proj = scatter_about(seeds[1], (F, C), F ** -0.5, 0.625, ((0, 2),))
    kernel = scatter_about(seeds[2], (LAYERS, C, 9), 0.4, 2.4, ((1, 2),), jnp.float32)
    mix = scatter_about(seeds[3], (LAYERS, C, C), C ** -0.5, 1.0, ((2, 2),))
    readout = scatter_about(seeds[4], (C,), C ** -0.5, 1.0, (), jnp.float32)
    dilations = draw_dilations(jax.random.fold_in(seeds[10], 71), part)
    chrom_lengths = draw_chrom_lengths(jax.random.fold_in(seeds[10], 71), part)
    pairs = draw_pairs(jax.random.fold_in(jax.random.fold_in(seeds[10], part), 71), part)
    contact_cot = scatter_about(own_keys[8], (BAND, BINS), 1.0, 6.0, ((0, 2), (1, 4)), jnp.float32)
    trans_cot = scatter_about(own_keys[9], (PAIRS, BIN_DEV, BIN_DEV), 1.0, 6.0, ((0, 4), (1, 4)), jnp.float32)
    return dict(features=features, proj=proj, kernel=kernel, mix=mix, readout=readout, dilations=dilations, chrom_lengths=chrom_lengths, pairs=pairs, contact_cot=contact_cot, trans_cot=trans_cot)


HIGHEST_PRECISION = lax.Precision.HIGHEST

def chrom_of(positions, chrom_lengths, bin_limit):
    chrom_ends = jnp.cumsum(chrom_lengths)
    chrom_ids = lax.optimization_barrier(jnp.sum((positions[..., None] >= chrom_ends).astype(jnp.int32), axis=-1))
    return jnp.where(positions < bin_limit, chrom_ids, -1)

def forward_pass(features_wide, proj_wide, kernel, mix_wide, readout, dilations, chrom_lengths, pairs):
    profile = jnp.dot(features_wide, proj_wide, precision=HIGHEST_PRECISION)
    offsets = jnp.arange(BAND, dtype=jnp.int32)
    positions = jnp.arange(BINS, dtype=jnp.int32)
    here_ids = chrom_of(positions, chrom_lengths, BINS)
    there_ids = chrom_of(positions[None, :] + offsets[:, None], chrom_lengths, BINS)
    band_mask = (here_ids[None, :] == there_ids).astype(jnp.float32)
    extended = jnp.concatenate([profile, jnp.zeros((BAND, C), jnp.float32)], axis=0).T
    shifted = jax.vmap(lambda offset_value: lax.dynamic_slice_in_dim(extended, offset_value, BINS, 1), out_axes=1)(offsets)
    pair_field = profile.T[:, None, :] * shifted * band_mask[None]
    for layer_id in range(LAYERS):
        dilation = dilations[layer_id]
        padded = jnp.pad(pair_field, ((0, 0), (DMAX, DMAX), (DMAX, DMAX)))
        mirrored = jnp.flip(padded[:, DMAX + 1:2 * DMAX + 1, :], axis=1)
        padded = jnp.concatenate([mirrored, padded[:, DMAX:, :]], axis=1)
        summed = jnp.zeros_like(pair_field)
        tap_index = 0
        for across in (-1, 0, 1):
            for along in (-1, 0, 1):
                corner = (jnp.int32(0), DMAX + along * dilation, DMAX + across * dilation)
                window = lax.dynamic_slice(padded, corner, pair_field.shape)
                summed = summed + kernel[layer_id, :, tap_index][:, None, None] * window
                tap_index += 1
        hidden = jax.nn.relu(summed).astype(jnp.bfloat16)
        update = jnp.einsum('ckn,ce->ekn', hidden.astype(jnp.float32), mix_wide[layer_id], precision=HIGHEST_PRECISION)
        pair_field = (pair_field + update) * band_mask[None]
    contact = jnp.einsum('c,ckn->kn', readout, pair_field, precision=HIGHEST_PRECISION)
    block_table = profile.reshape(BLOCKS, BIN_DEV, C)
    block_ids = here_ids.reshape(BLOCKS, BIN_DEV)
    first_rows = block_table[pairs[:, 0]]
    second_rows = block_table[pairs[:, 1]]
    cross_mask = (block_ids[pairs[:, 0]][:, :, None] != block_ids[pairs[:, 1]][:, None, :]).astype(jnp.float32)
    trans_maps = jnp.einsum('prc,psc->prs', first_rows * readout, second_rows, precision=HIGHEST_PRECISION) * cross_mask
    return (contact, trans_maps)

def reference(features, proj, kernel, mix, readout, dilations, chrom_lengths, pairs, contact_cot, trans_cot):

    def run_model(features_wide, proj_wide, kernel_taps, mix_wide):
        return forward_pass(features_wide, proj_wide, kernel_taps, mix_wide, readout, dilations, chrom_lengths, pairs)
    outputs, pullback = jax.vjp(run_model, features.astype(jnp.float32), proj.astype(jnp.float32), kernel, mix.astype(jnp.float32))
    grads = pullback((contact_cot, trans_cot))
    return (outputs[0], outputs[1], grads[0], grads[1], grads[2], grads[3])
```

```python
import jax
import jax.numpy as jnp
from jax import lax
from jax.experimental import pallas as pl
from jax.experimental.pallas import tpu as pltpu
from jax.sharding import PartitionSpec as P

HALO = 8
LANES = 128
GUARD = 32
LOW = 16
BATCH = 8
EXACT = lax.Precision.HIGHEST
NT = (((1,), (1,)), ((), ()))
NN = (((1,), (0,)), ((), ()))


def mm(a, b, dims=NN, precision=None):
    return lax.dot_general(a, b, dims, precision=precision, preferred_element_type=jnp.float32)


def split(value):
    high = value.astype(jnp.bfloat16)
    return high, (value - high.astype(jnp.float32)).astype(jnp.bfloat16)


def band_kernel(
    dil, chroms, pairs, feats, proj, proj_t, mix, mix_t, taps_in, ro_col, ro_row, cot, tcot,
    contact, maps, grads, gproj_t, gtaps, gmix,
    taps, spread, env, prof, prof_t, x0, x1, h, go, gs, gf, go1, gs1, gpad, acc, spent,
):
    chans = proj.shape[1]
    layers = mix.shape[0]
    bin_dev = LANES
    seq_count, chan_count = lax.axis_size("seq"), lax.axis_size("chan")
    seq_pos, chan_pos, sub_pos = lax.axis_index("seq"), lax.axis_index("chan"), lax.axis_index("sub")
    total = seq_count * bin_dev
    own_bins = bin_dev // chan_count
    rows = h.shape[1]
    own_rows = rows - 3 * HALO
    wide = BATCH * chans
    first = seq_pos * bin_dev + chan_pos * own_bins - GUARD
    k_base = sub_pos * (own_rows - 3 * HALO)
    own_start = sub_pos * 3 * HALO
    is_low = (sub_pos == 0).astype(jnp.float32)

    ends, run = [], jnp.int32(0)
    for j in range(chroms.shape[0]):
        run = run + chroms[j]
        ends.append(run)

    def end_of(pos):
        best = jnp.full(pos.shape, 1 << 20, jnp.int32)
        for e in ends:
            best = jnp.minimum(best, jnp.where(pos < e, e, 1 << 20))
        return best

    pos = first + lax.broadcasted_iota(jnp.int32, (1, LANES), 1)
    left = jnp.where((pos >= 0) & (pos < total), end_of(pos) - pos, 0)
    lane = lax.broadcasted_iota(jnp.int32, (1, LANES), 1)
    own_lane = ((lane >= GUARD) & (lane < GUARD + own_bins)).astype(jnp.float32)

    def mask(r):
        return (k_base + r < left).astype(jnp.float32)

    r_i = lax.broadcasted_iota(jnp.int32, (wide, chans), 0)
    c_i = lax.broadcasted_iota(jnp.int32, (wide, chans), 1)
    fan = (lax.rem(r_i, chans) == c_i).astype(jnp.bfloat16)
    r_w = lax.broadcasted_iota(jnp.int32, (wide, wide), 0) // chans
    c_w = lax.broadcasted_iota(jnp.int32, (wide, wide), 1) // chans
    diag = r_w == c_w
    for l in range(layers):
        for side, source in enumerate((mix_t, mix)):
            tall = mm(fan, source[l]).astype(jnp.bfloat16)
            full = mm(tall, fan, NT)
            spread[2 * l + side] = jnp.where(diag, full, 0.0).astype(jnp.bfloat16)
        for t in range(9):
            taps[l, t] = jnp.broadcast_to(taps_in[l][:, t : t + 1], (chans, LANES))

    prof[...] = mm(feats[pl.ds(LANES, total), :], proj[...])
    for b in range(seq_count):
        prof_t[b] = mm(proj_t[...], feats[(b + 1) * LANES : (b + 2) * LANES, :], NT)
    start = pl.multiple_of(first + LANES, 16)
    env[...] = mm(proj_t[...], feats[pl.ds(start, 2 * LANES), :], NT)
    ro = jnp.broadcast_to(ro_col[...], (chans, LANES))

    for buf in (x0, x1, gs, gs1):
        for r in (*range(LOW), *range(LOW + rows, 2 * LOW + rows)):
            buf[r] = jnp.zeros((chans, LANES), jnp.float32)

    def clear(i, _):
        gs[LOW + i] = jnp.zeros((chans, LANES), jnp.float32)
        gs1[LOW + i] = jnp.zeros((chans, LANES), jnp.float32)
        go1[i] = jnp.zeros((chans, LANES), jnp.float32)
        return 0

    lax.fori_loop(0, rows, clear, 0, unroll=4)

    def build(i, _):
        k = k_base + i
        moved = pltpu.roll(env[...], lax.rem(2 * LANES - k, 2 * LANES), 1)[:, :LANES]
        x0[LOW + i] = env[:, :LANES] * moved * mask(i)
        return 0

    lax.fori_loop(0, rows, build, 0, unroll=4)

    def conv(x, l, d, r, sign):
        lines = [x[LOW + r + sign * b * d] for b in (-1, 0, 1)]
        sums = []
        for a in range(3):
            t = [taps[l, 3 * a + b] * lines[b] for b in range(3)]
            sums.append(t[0] + t[1] + t[2])
        fwd, back = (d, LANES - d) if sign > 0 else (LANES - d, d)
        return sums[1] + pltpu.roll(sums[0], fwd, 1) + pltpu.roll(sums[2], back, 1)

    xs = [x0, x1]
    for l in range(layers):
        d = dil[l]
        x = xs[l]
        for m in range(1, HALO + 1):
            x[LOW - m] = x[LOW + m]
        base = sub_pos * HALO * (l + 1)

        def layer(i, _, l=l, d=d, x=x, base=base):
            r0 = base + i * BATCH
            for j in range(BATCH):
                summed = conv(x, l, d, r0 + j, 1)
                h[l, r0 + j] = jnp.maximum(summed, 0.0).astype(jnp.bfloat16)
            upd = mm(spread[2 * l], h[l, pl.ds(r0, BATCH)].reshape(wide, LANES))
            upd = upd.reshape(BATCH, chans, LANES)
            for j in range(BATCH):
                new = (x[LOW + r0 + j] + upd[j]) * mask(r0 + j)
                if l + 1 < layers:
                    xs[l + 1][LOW + r0 + j] = new
                else:
                    contact[pl.ds(i * BATCH + j, 1), :] = jnp.sum(new * ro, axis=0, keepdims=True)
            return 0

        lax.fori_loop(0, (rows - HALO * (l + 1)) // BATCH, layer, 0)

    def pull(l, r0, source, target):
        g = source[pl.ds(r0, BATCH)].reshape(wide, LANES)
        high, low = split(g)
        gh = mm(spread[2 * l + 1], high) + mm(spread[2 * l + 1], low)
        gh = gh.astype(jnp.bfloat16).astype(jnp.float32).reshape(BATCH, chans, LANES)
        for j in range(BATCH):
            on = h[l, r0 + j].astype(jnp.float32) > 0
            target[LOW + r0 + j] = jnp.where(on, gh[j], 0.0)

    def weight_grads(l, x, d, g_out, g_sum):
        acc[...] = jnp.zeros_like(acc)

        def body(i, sums):
            r0 = own_start + i * BATCH
            g = (g_out[pl.ds(r0, BATCH)] * own_lane).astype(jnp.bfloat16).reshape(wide, LANES)
            acc[...] += mm(h[l, pl.ds(r0, BATCH)].reshape(wide, LANES), g, NT)
            for j in range(BATCH):
                r = r0 + j
                g0 = g_sum[LOW + r] * own_lane
                moved = (pltpu.roll(g0, LANES - d, 1), g0, pltpu.roll(g0, d, 1))
                lines = [x[LOW + r + b * d] for b in (-1, 0, 1)]
                sums = tuple(sums[t] + moved[t // 3] * lines[t % 3] for t in range(9))
            return sums

        zero = jnp.zeros((chans, LANES), jnp.float32)
        sums = lax.fori_loop(0, own_rows // BATCH, body, (zero,) * 9)
        for t in range(9):
            gtaps[l, :, t : t + 1] = jnp.sum(sums[t], axis=1, keepdims=True)
        tall = jnp.sum(jnp.where(diag, acc[...], 0.0).reshape(BATCH, chans, wide), axis=0)
        gmix[l] = mm(tall, fan.astype(jnp.float32), precision=EXACT)

    def last_out(i, _):
        r0 = sub_pos * 2 * HALO + i * BATCH
        for j in range(BATCH):
            line = cot[pl.ds(i * BATCH + j, 1), :] * mask(r0 + j)
            go[r0 + j] = ro * line
        pull(1, r0, go, gs)
        return 0

    lax.fori_loop(0, (rows - 2 * HALO) // BATCH, last_out, 0)
    weight_grads(1, x1, dil[1], go, gs)

    def fold(l, d, g, target):
        for m in range(1, HALO + 1):
            target[m] = target[m] + is_low * conv(g, l, d, -m, -1)

    def back_field(i, _):
        r0 = own_start + i * BATCH
        for j in range(BATCH):
            gf[r0 + j] = go[r0 + j] + conv(gs, 1, dil[1], r0 + j, -1)
        return 0

    lax.fori_loop(0, own_rows // BATCH, back_field, 0)
    fold(1, dil[1], gs, gf)

    def first_out(i, _):
        r0 = own_start + i * BATCH
        for j in range(BATCH):
            go1[r0 + j] = gf[r0 + j] * (mask(r0 + j) * own_lane)
        pull(0, r0, go1, gs1)
        return 0

    lax.fori_loop(0, own_rows // BATCH, first_out, 0)
    weight_grads(0, x0, dil[0], go1, gs1)

    def back_first(i, _):
        r0 = sub_pos * 2 * HALO + i * BATCH
        for j in range(BATCH):
            gf[r0 + j] = go1[r0 + j] + conv(gs1, 0, dil[0], r0 + j, -1)
        return 0

    lax.fori_loop(0, (rows - 2 * HALO) // BATCH, back_first, 0)
    fold(0, dil[0], gs1, gf)

    def to_profile(i, carry):
        near, far = carry
        r = sub_pos * 2 * HALO + i
        k = k_base + r
        g = gf[r] * mask(r)
        moved = pltpu.roll(env[...], lax.rem(2 * LANES - k, 2 * LANES), 1)[:, :LANES]
        near = near + g * moved
        part = jnp.concatenate([g * env[:, :LANES], jnp.zeros((chans, LANES), jnp.float32)], axis=1)
        far = far + pltpu.roll(part, k, 1)
        return near, far

    near, far = lax.fori_loop(
        0, rows - 2 * HALO, to_profile,
        (jnp.zeros((chans, LANES), jnp.float32), jnp.zeros((chans, 2 * LANES), jnp.float32)),
    )
    near = far[:, :LANES] + near
    zero = jnp.zeros((chans, LANES), jnp.float32)
    whole = jnp.concatenate([near, far[:, LANES:], zero], axis=1)
    place = first + LANES
    tile = place // LANES
    whole = pltpu.roll(whole, lax.rem(place, LANES), 1)
    for b in range(gpad.shape[0]):
        gpad[b] = zero
    for b in range(3):
        gpad[tile + b] = whole[:, b * LANES : (b + 1) * LANES]

    rows_trans = tcot.shape[1]
    row_start = pl.multiple_of((chan_pos * 2 + sub_pos) * rows_trans, 8)
    for n in range(tcot.shape[0]):
        p, q = pairs[n, 0], pairs[n, 1]
        first_rows = prof[pl.ds(pl.multiple_of(p * LANES + row_start, 8), rows_trans), :] * ro_row[...]
        second = prof[pl.ds(pl.multiple_of(q * LANES, 8), LANES), :]
        row_pos = p * LANES + row_start + lax.broadcasted_iota(jnp.int32, (rows_trans, LANES), 0)
        col_pos = q * LANES + lax.broadcasted_iota(jnp.int32, (rows_trans, LANES), 1)
        cross = (end_of(row_pos) != end_of(col_pos)).astype(jnp.float32)
        maps[n] = mm(first_rows, second, NT, EXACT) * cross
        spent[...] = jnp.zeros_like(spent)
        spent[pl.ds(row_start, rows_trans), :] = tcot[n] * cross
        to_first = mm(prof_t[q], spent[...], NT, EXACT) * ro
        to_second = mm(prof_t[p] * ro, spent[...], NN, EXACT)
        gpad[1 + p] = gpad[1 + p] + to_first
        gpad[1 + q] = gpad[1 + q] + to_second

    total_proj = jnp.zeros(gproj_t.shape, jnp.float32)
    for b in range(seq_count):
        g = gpad[1 + b]
        grads[b] = g
        high, low = split(g)
        block = feats[(b + 1) * LANES : (b + 2) * LANES, :]
        total_proj = total_proj + mm(high, block) + mm(low, block)
    gproj_t[...] = total_proj


def per_device(
    features, proj, kernel, mix, readout, dilations, chrom_lengths, pairs, contact_cot, trans_cot
):
    bin_dev = features.shape[0]
    chans = proj.shape[1]
    band_dev = contact_cot.shape[0]
    layers = kernel.shape[0]
    seq_count, chan_count = lax.axis_size("seq"), lax.axis_size("chan")
    seq_pos, chan_pos, sub_pos = lax.axis_index("seq"), lax.axis_index("chan"), lax.axis_index("sub")
    own_bins = bin_dev // chan_count
    total = bin_dev * seq_count
    rows = band_dev + 3 * HALO

    feats = lax.all_gather(features, ("seq", "chan"), axis=0)
    feats = feats.reshape(seq_count, chan_count, bin_dev, -1).transpose(0, 2, 1, 3)
    feats = jnp.pad(feats.reshape(total, -1), ((bin_dev, 2 * bin_dev), (0, 0)))
    proj_all = lax.all_gather(proj, "chan", axis=0, tiled=True)
    mix_all = lax.all_gather(mix, "chan", axis=2, tiled=True)
    taps = lax.all_gather(kernel, "chan", axis=1, tiled=True)
    edge = jnp.where(sub_pos == 0, contact_cot[-HALO:], contact_cot[:HALO])
    edge = lax.ppermute(edge, "sub", [(0, 1), (1, 0)])
    zeros = jnp.zeros_like(edge)
    cot = jnp.where(
        sub_pos == 0,
        jnp.concatenate([contact_cot, edge], axis=0),
        jnp.concatenate([edge, contact_cot], axis=0),
    )
    side = jnp.where(chan_pos == 0, cot[:, -HALO:], cot[:, :HALO])
    moves = []
    for s in range(seq_count - 1):
        moves.append((s * chan_count, (s + 1) * chan_count))
        moves.append(((s + 2) * chan_count - 1, (s + 1) * chan_count - 1))
    side = lax.ppermute(side, ("seq", "chan"), moves)
    blank = jnp.zeros((cot.shape[0], GUARD - HALO), jnp.float32)
    cot = jnp.concatenate([blank, side, cot, side, blank], axis=1)
    cot = lax.dynamic_slice_in_dim(cot, chan_pos * own_bins, LANES, 1)

    f32 = jnp.float32
    smem = pl.BlockSpec(memory_space=pltpu.SMEM)
    vmem = pl.BlockSpec(memory_space=pltpu.VMEM)
    field = pltpu.VMEM((2 * LOW + rows, chans, LANES), f32)
    plain = pltpu.VMEM((rows, chans, LANES), f32)
    wide = BATCH * chans
    width = proj_all.shape[0]
    contact, maps, grads, gproj_t, gtaps, gmix = pl.pallas_call(
        band_kernel,
        out_shape=(
            jax.ShapeDtypeStruct((band_dev + HALO, LANES), f32),
            jax.ShapeDtypeStruct(trans_cot.shape, f32),
            jax.ShapeDtypeStruct((seq_count, chans, LANES), f32),
            jax.ShapeDtypeStruct((chans, width), f32),
            jax.ShapeDtypeStruct((layers, chans, 9), f32),
            jax.ShapeDtypeStruct((layers, chans, chans), f32),
        ),
        in_specs=[smem] * 3 + [vmem] * 10,
        out_specs=(vmem,) * 6,
        scratch_shapes=[
            pltpu.VMEM((layers, 9, chans, LANES), f32),
            pltpu.VMEM((2 * layers, wide, wide), jnp.bfloat16),
            pltpu.VMEM((chans, 2 * LANES), f32),
            pltpu.VMEM((total, chans), f32),
            pltpu.VMEM((seq_count, chans, LANES), f32),
            field,
            field,
            pltpu.VMEM((layers, rows, chans, LANES), jnp.bfloat16),
            plain,
            field,
            plain,
            plain,
            field,
            pltpu.VMEM((seq_count + 3, chans, LANES), f32),
            pltpu.VMEM((wide, wide), f32),
            pltpu.VMEM((LANES, LANES), f32),
        ],
        compiler_params=pltpu.CompilerParams(vmem_limit_bytes=48 * 1024 * 1024),
    )(
        dilations, chrom_lengths, pairs, feats, proj_all, proj_all.T, mix_all,
        mix_all.transpose(0, 2, 1), taps, readout[:, None], readout[None, :], cot, trans_cot,
    )
    everyone = ("seq", "chan", "sub")
    grads, gproj_t, gtaps, gmix = lax.psum((grads, gproj_t, gtaps, gmix), everyone)
    own = lax.dynamic_index_in_dim(grads, seq_pos, 0, keepdims=False)
    grad_features = lax.dot_general(
        own, proj.astype(f32), (((0,), (1,)), ((), ())), precision=EXACT
    )
    chan_dev, width_dev = kernel.shape[1], proj.shape[0]
    grad_proj = lax.dynamic_slice_in_dim(gproj_t, chan_pos * width_dev, width_dev, 1).T
    grad_kernel = lax.dynamic_slice_in_dim(gtaps, chan_pos * chan_dev, chan_dev, 1)
    grad_mix = lax.dynamic_slice_in_dim(gmix, chan_pos * chan_dev, chan_dev, 2)
    contact = lax.dynamic_slice(
        contact, (sub_pos * HALO, jnp.int32(GUARD)), (band_dev, own_bins)
    )
    contact = lax.all_gather(contact, "chan", axis=1, tiled=True)
    return (contact, maps, grad_features, grad_proj, grad_kernel, grad_mix)


def solution(mesh):
    in_specs = (
        P(("groups", "seq"), "chan"),
        P("chan", None),
        P(None, "chan", None),
        P(None, None, "chan"),
        P(),
        P(),
        P(),
        P(("groups", "seq"), None),
        P("sub", ("groups", "seq")),
        P(("groups", "seq"), ("chan", "sub"), None),
    )
    out_specs = (
        P("sub", ("groups", "seq")),
        P(("groups", "seq"), ("chan", "sub"), None),
        P(("groups", "seq"), "chan"),
        P(("groups", "chan"), None),
        P("groups", "chan", None),
        P("groups", None, "chan"),
    )
    return jax.shard_map(
        per_device, mesh=mesh, in_specs=in_specs, out_specs=out_specs, check_vma=False
    )
```

```python
import jax
import jax.numpy as jnp
from jax import lax
from jax.experimental import pallas as pl
from jax.experimental.pallas import tpu as pltpu
from jax.sharding import PartitionSpec as P

HALO = 8
LANES = 128
GUARD = 32
LOW = 16
BATCH = 8
MESH = pl.DeviceIdType.MESH
EXACT = lax.Precision.HIGHEST
NT = (((1,), (1,)), ((), ()))
NN = (((1,), (0,)), ((), ()))


def mm(a, b, dims=NN, precision=None):
    return lax.dot_general(a, b, dims, precision=precision, preferred_element_type=jnp.float32)


def split(value):
    high = value.astype(jnp.bfloat16)
    return high, (value - high.astype(jnp.float32)).astype(jnp.bfloat16)


def place():
    return lax.axis_index("seq"), lax.axis_index("chan"), lax.axis_index("sub")


def meet(sources, target_count):
    barrier = pltpu.get_barrier_semaphore()
    for device in sources:
        pl.semaphore_signal(barrier, inc=1, device_id=device, device_id_type=MESH)
    pl.semaphore_wait(barrier, target_count)


def at(s, x, u):
    return {"seq": s, "chan": x, "sub": u}


def gather_kernel(
    features, proj_t, mix, taps, cot,
    feats, projs, mixes, taps_all, edge, side, side_edge,
    send_feats, recv_feats, send_small, recv_small, send_cot, recv_cot,
):
    seq_count, chan_count = lax.axis_size("seq"), lax.axis_size("chan")
    s, x, u = place()
    bins = features.shape[0]
    band = cot.shape[0]
    peers, sources = [], []
    for ds in range(seq_count):
        for dx in range(chan_count):
            if ds or dx:
                peers.append(at(lax.rem(s + ds, seq_count), lax.rem(x + dx, chan_count), u))
                back = (lax.rem(s + seq_count - ds, seq_count), lax.rem(x + chan_count - dx, chan_count))
                sources.append(at(*back, u))
    step = jnp.where(x == 0, 1, seq_count - 1)
    ahead = lax.rem(s + step, seq_count)
    behind = lax.rem(s + seq_count - step, seq_count)
    other = 1 - u
    meet(sources + [at(s, x, other), at(behind, x, other)], len(peers) + 2)

    copies = []

    def push(source, target, sems, j, device):
        copy = pltpu.make_async_remote_copy(
            src_ref=source, dst_ref=target, send_sem=sems[0].at[j], recv_sem=sems[1].at[j],
            device_id=device, device_id_type=MESH,
        )
        copy.start()
        copies.append(copy)

    slot = pl.ds(pl.multiple_of((1 + s) * bins, bins), bins)
    rim = pl.ds(pl.multiple_of((1 - u) * (band - HALO), HALO), HALO)
    for j, device in enumerate(peers):
        push(features, feats.at[x, slot], (send_feats, recv_feats), j, device)
    push(cot, side, (send_cot, recv_cot), 0, at(ahead, x, u))
    push(cot.at[rim], side_edge, (send_cot, recv_cot), 1, at(ahead, x, other))
    push(cot.at[rim], edge, (send_cot, recv_cot), 2, at(s, x, other))
    for dx in range(1, chan_count):
        device = at(s, lax.rem(x + dx, chan_count), u)
        small = (send_small, recv_small)
        push(proj_t, projs.at[x], small, 3 * dx - 3, device)
        push(mix, mixes.at[x], small, 3 * dx - 2, device)
        push(taps, taps_all.at[x], small, 3 * dx - 1, device)
    feats[x, slot] = features[...]
    projs[x] = proj_t[...]
    mixes[x] = mix[...]
    taps_all[x] = taps[...]
    for c in range(chan_count):
        feats[c, :bins] = jnp.zeros((bins, features.shape[1]), features.dtype)
        feats[c, (1 + seq_count) * bins :] = jnp.zeros((2 * bins, features.shape[1]), features.dtype)
    for copy in copies:
        copy.wait()


def reduce_kernel(
    part, misc, contact, proj_t,
    contact_out, grad_features, grad_proj, grad_kernel, grad_mix,
    parts, miscs, contacts, outgoing, arrived, taps_sum, send_a, recv_a, send_b, recv_b, send_c, recv_c,
):
    seq_count, chan_count = lax.axis_size("seq"), lax.axis_size("chan")
    s, x, u = place()
    layers, chan_dev = grad_kernel.shape[0], grad_kernel.shape[1]
    width = proj_t.shape[1]
    far = [lax.rem(s + j, seq_count) for j in range(1, seq_count)]
    near = [(dx, du) for dx in range(chan_count) for du in range(2) if dx or du]

    def neighbour(dx, du):
        return lax.rem(x + dx, chan_count), lax.rem(u + du, 2)

    everyone = [at(t, x, u) for t in far] + [at(s, *neighbour(dx, du)) for dx, du in near]
    meet(everyone, len(everyone))
    copies = []

    def push(source, target, sems, j, device):
        copy = pltpu.make_async_remote_copy(
            src_ref=source, dst_ref=target, send_sem=sems[0].at[j], recv_sem=sems[1].at[j],
            device_id=device, device_id_type=MESH,
        )
        copy.start()
        return copy

    first = []
    for j, t in enumerate(far):
        first.append(push(misc, miscs.at[s], (send_a, recv_a), 2 * j, at(t, x, u)))
        first.append(push(part.at[t], parts.at[s], (send_a, recv_a), 2 * j + 1, at(t, x, u)))
    shown = []
    for dx in range(1, chan_count):
        device = at(s, lax.rem(x + dx, chan_count), u)
        shown.append(push(contact, contacts.at[x], (send_c, recv_c), dx - 1, device))
    parts[s] = part[s]
    miscs[s] = misc[...]
    contacts[x] = contact[...]
    for copy in first:
        copy.wait()
    f32 = jnp.float32
    total = parts[0].astype(f32)
    for t in range(1, seq_count):
        total = total + parts[t].astype(f32)
    for c in range(chan_count):
        outgoing[c, 0] = total
        rest = miscs[0, c].astype(f32)
        for t in range(1, seq_count):
            rest = rest + miscs[t, c].astype(f32)
        outgoing[c, 1] = rest
    second = []
    for j, (dx, du) in enumerate(near):
        nx, nu = neighbour(dx, du)
        second.append(
            push(outgoing.at[nx], arrived.at[2 * x + u], (send_b, recv_b), j, at(s, nx, nu))
        )
    arrived[2 * x + u] = outgoing[x]
    for copy in shown:
        copy.wait()
    picture = contacts[0]
    for c in range(1, chan_count):
        picture = picture + contacts[c]
    contact_out[...] = picture
    for copy in second:
        copy.wait()
    total, rest = arrived[0, 0], arrived[0, 1]
    for j in range(1, 2 * chan_count):
        total, rest = total + arrived[j, 0], rest + arrived[j, 1]
    grad_features[...] = mm(total.T, proj_t[...].astype(f32), NN, EXACT)
    grad_proj[...] = rest.T[:width]
    for l in range(layers):
        grad_mix[l] = rest[:, width + l * chan_dev : width + (l + 1) * chan_dev]
        off = width + layers * chan_dev + 9 * l
        taps_sum[...] = rest
        grad_kernel[l] = taps_sum[pl.ds(x * chan_dev, chan_dev), off : off + 9]


def band_kernel(
    dil, chroms, pairs, feats, projs, mixes, taps_in, ro_col, ro_row,
    cot_own, cot_edge, cot_side, cot_side_edge, tcot,
    contact, maps, part, misc,
    taps, spread, env, prof, prof_t, x0, x1, h, go, gs, gf, go1, gs1, gpad, acc, spent, cot, picture, rest,
):
    chans, width = projs.shape[1:]
    layers, chan_dev = mixes.shape[1], mixes.shape[3]
    bin_dev = LANES
    seq_count, chan_count = lax.axis_size("seq"), lax.axis_size("chan")
    seq_pos, chan_pos, sub_pos = place()
    total = seq_count * bin_dev
    own_bins = bin_dev // chan_count
    rows = h.shape[1]
    own_rows = rows - 3 * HALO
    wide = BATCH * chans
    first = seq_pos * bin_dev + chan_pos * own_bins - GUARD
    k_base = sub_pos * (own_rows - 3 * HALO)
    own_start = sub_pos * 3 * HALO
    is_low = (sub_pos == 0).astype(jnp.float32)

    ends, run = [], jnp.int32(0)
    for j in range(chroms.shape[0]):
        run = run + chroms[j]
        ends.append(run)

    def end_of(pos):
        best = jnp.full(pos.shape, 1 << 20, jnp.int32)
        for e in ends:
            best = jnp.minimum(best, jnp.where(pos < e, e, 1 << 20))
        return best

    pos = first + lax.broadcasted_iota(jnp.int32, (1, LANES), 1)
    left = jnp.where((pos >= 0) & (pos < total), end_of(pos) - pos, 0)
    lane = lax.broadcasted_iota(jnp.int32, (1, LANES), 1)
    own_lane = ((lane >= GUARD) & (lane < GUARD + own_bins)).astype(jnp.float32)

    def mask(r):
        return (k_base + r < left).astype(jnp.float32)

    r_i = lax.broadcasted_iota(jnp.int32, (wide, chans), 0)
    c_i = lax.broadcasted_iota(jnp.int32, (wide, chans), 1)
    fan = (lax.rem(r_i, chans) == c_i).astype(jnp.bfloat16)
    r_w = lax.broadcasted_iota(jnp.int32, (wide, wide), 0) // chans
    c_w = lax.broadcasted_iota(jnp.int32, (wide, wide), 1) // chans
    diag = r_w == c_w
    for l in range(layers):
        mixed = jnp.concatenate([mixes[c, l] for c in range(chan_count)], axis=1)
        for side, dims in enumerate((NT, NN)):
            tall = mm(fan, mixed, dims).astype(jnp.bfloat16)
            full = mm(tall, fan, NT)
            spread[2 * l + side] = jnp.where(diag, full, 0.0).astype(jnp.bfloat16)
        for t in range(9):
            for c in range(chan_count):
                column = taps_in[c, l][:, t : t + 1]
                taps[l, t, c * chan_dev : (c + 1) * chan_dev, :] = jnp.broadcast_to(
                    column, (chan_dev, LANES)
                )

    turn = lax.rem(LANES + GUARD - chan_pos * own_bins, LANES)
    column = lane - GUARD + chan_pos * own_bins
    inside = (column >= 0) & (column < LANES)
    own_at = pl.multiple_of(sub_pos * HALO, HALO)
    lines = [
        jnp.where(inside, pltpu.roll(here[...], turn, 1), pltpu.roll(there[...], turn, 1))
        for here, there in ((cot_own, cot_side), (cot_edge, cot_side_edge))
    ]
    cot[...] = jnp.where(
        sub_pos == 0,
        jnp.concatenate(lines, axis=0),
        jnp.concatenate(lines[::-1], axis=0),
    )

    def project(rows_at, count):
        sums = [mm(projs[c], feats[c, pl.ds(rows_at, count), :], NT) for c in range(chan_count)]
        return sum(sums[1:], sums[0])

    for b in range(seq_count):
        block = [feats[c, (b + 1) * LANES : (b + 2) * LANES, :] for c in range(chan_count)]
        sums = [mm(block[c], projs[c], NT) for c in range(chan_count)]
        prof[b * LANES : (b + 1) * LANES, :] = sum(sums[1:], sums[0])
        prof_t[b] = project((b + 1) * LANES, LANES)
    env[...] = project(pl.multiple_of(first + LANES, 16), 2 * LANES)
    ro = jnp.broadcast_to(ro_col[...], (chans, LANES))

    for buf in (x0, x1, gs, gs1):
        for r in (*range(LOW), *range(LOW + rows, 2 * LOW + rows)):
            buf[r] = jnp.zeros((chans, LANES), jnp.float32)

    def clear(i, _):
        gs[LOW + i] = jnp.zeros((chans, LANES), jnp.float32)
        gs1[LOW + i] = jnp.zeros((chans, LANES), jnp.float32)
        go1[i] = jnp.zeros((chans, LANES), jnp.float32)
        return 0

    lax.fori_loop(0, rows, clear, 0, unroll=4)

    def build(i, _):
        k = k_base + i
        moved = pltpu.roll(env[...], lax.rem(2 * LANES - k, 2 * LANES), 1)[:, :LANES]
        x0[LOW + i] = env[:, :LANES] * moved * mask(i)
        return 0

    lax.fori_loop(0, rows, build, 0, unroll=4)

    def conv(x, l, d, r, sign):
        lines = [x[LOW + r + sign * b * d] for b in (-1, 0, 1)]
        sums = []
        for a in range(3):
            t = [taps[l, 3 * a + b] * lines[b] for b in range(3)]
            sums.append(t[0] + t[1] + t[2])
        fwd, back = (d, LANES - d) if sign > 0 else (LANES - d, d)
        return sums[1] + pltpu.roll(sums[0], fwd, 1) + pltpu.roll(sums[2], back, 1)

    xs = [x0, x1]
    for l in range(layers):
        d = dil[l]
        x = xs[l]
        for m in range(1, HALO + 1):
            x[LOW - m] = x[LOW + m]
        base = sub_pos * HALO * (l + 1)

        def layer(i, _, l=l, d=d, x=x, base=base):
            r0 = base + i * BATCH
            for j in range(BATCH):
                summed = conv(x, l, d, r0 + j, 1)
                h[l, r0 + j] = jnp.maximum(summed, 0.0).astype(jnp.bfloat16)
            upd = mm(spread[2 * l], h[l, pl.ds(r0, BATCH)].reshape(wide, LANES))
            upd = upd.reshape(BATCH, chans, LANES)
            for j in range(BATCH):
                new = (x[LOW + r0 + j] + upd[j]) * mask(r0 + j)
                if l + 1 < layers:
                    xs[l + 1][LOW + r0 + j] = new
                else:
                    picture[pl.ds(i * BATCH + j, 1), :] = jnp.sum(new * ro, axis=0, keepdims=True)
            return 0

        lax.fori_loop(0, (rows - HALO * (l + 1)) // BATCH, layer, 0)

    shown = picture[pl.ds(own_at, own_rows), :] * own_lane
    contact[...] = pltpu.roll(shown, lax.rem(LANES - turn, LANES), 1)
    for c in range(chan_count):
        rest[c] = jnp.zeros((chans, LANES), jnp.float32)

    def pull(l, r0, source, target):
        g = source[pl.ds(r0, BATCH)].reshape(wide, LANES)
        high, low = split(g)
        gh = mm(spread[2 * l + 1], high) + mm(spread[2 * l + 1], low)
        gh = gh.astype(jnp.bfloat16).astype(jnp.float32).reshape(BATCH, chans, LANES)
        for j in range(BATCH):
            on = h[l, r0 + j].astype(jnp.float32) > 0
            target[LOW + r0 + j] = jnp.where(on, gh[j], 0.0)

    def weight_grads(l, x, d, g_out, g_sum):
        acc[...] = jnp.zeros_like(acc)

        def body(i, sums):
            r0 = own_start + i * BATCH
            g = (g_out[pl.ds(r0, BATCH)] * own_lane).astype(jnp.bfloat16).reshape(wide, LANES)
            acc[...] += mm(h[l, pl.ds(r0, BATCH)].reshape(wide, LANES), g, NT)
            for j in range(BATCH):
                r = r0 + j
                g0 = g_sum[LOW + r] * own_lane
                moved = (pltpu.roll(g0, LANES - d, 1), g0, pltpu.roll(g0, d, 1))
                lines = [x[LOW + r + b * d] for b in (-1, 0, 1)]
                sums = tuple(sums[t] + moved[t // 3] * lines[t % 3] for t in range(9))
            return sums

        zero = jnp.zeros((chans, LANES), jnp.float32)
        sums = lax.fori_loop(0, own_rows // BATCH, body, (zero,) * 9)
        tile = jnp.zeros((chans, LANES), jnp.float32)
        for t in range(9):
            line = jnp.sum(sums[t], axis=1, keepdims=True)
            off = width + layers * chan_dev + 9 * l + t
            tile = tile + jnp.where(lane == off, line, 0.0)
        tall = jnp.sum(jnp.where(diag, acc[...], 0.0).reshape(BATCH, chans, wide), axis=0)
        row_e = lax.rem(lax.broadcasted_iota(jnp.int32, (wide, LANES), 0), chans)
        col_e = lax.broadcasted_iota(jnp.int32, (wide, LANES), 1) - width - l * chan_dev
        for c in range(chan_count):
            hit = (col_e >= 0) & (col_e < chan_dev) & (row_e == col_e + c * chan_dev)
            rest[c] = rest[c] + tile + mm(tall, hit.astype(jnp.float32), precision=EXACT)

    def last_out(i, _):
        r0 = sub_pos * 2 * HALO + i * BATCH
        for j in range(BATCH):
            line = cot[pl.ds(i * BATCH + j, 1), :] * mask(r0 + j)
            go[r0 + j] = ro * line
        pull(1, r0, go, gs)
        return 0

    lax.fori_loop(0, (rows - 2 * HALO) // BATCH, last_out, 0)
    weight_grads(1, x1, dil[1], go, gs)

    def fold(l, d, g, target):
        for m in range(1, HALO + 1):
            target[m] = target[m] + is_low * conv(g, l, d, -m, -1)

    def back_field(i, _):
        r0 = own_start + i * BATCH
        for j in range(BATCH):
            gf[r0 + j] = go[r0 + j] + conv(gs, 1, dil[1], r0 + j, -1)
        return 0

    lax.fori_loop(0, own_rows // BATCH, back_field, 0)
    fold(1, dil[1], gs, gf)

    def first_out(i, _):
        r0 = own_start + i * BATCH
        for j in range(BATCH):
            go1[r0 + j] = gf[r0 + j] * (mask(r0 + j) * own_lane)
        pull(0, r0, go1, gs1)
        return 0

    lax.fori_loop(0, own_rows // BATCH, first_out, 0)
    weight_grads(0, x0, dil[0], go1, gs1)

    def back_first(i, _):
        r0 = sub_pos * 2 * HALO + i * BATCH
        for j in range(BATCH):
            gf[r0 + j] = go1[r0 + j] + conv(gs1, 0, dil[0], r0 + j, -1)
        return 0

    lax.fori_loop(0, (rows - 2 * HALO) // BATCH, back_first, 0)
    fold(0, dil[0], gs1, gf)

    def to_profile(i, carry):
        near, far = carry
        r = sub_pos * 2 * HALO + i
        k = k_base + r
        g = gf[r] * mask(r)
        moved = pltpu.roll(env[...], lax.rem(2 * LANES - k, 2 * LANES), 1)[:, :LANES]
        near = near + g * moved
        part = jnp.concatenate([g * env[:, :LANES], jnp.zeros((chans, LANES), jnp.float32)], axis=1)
        far = far + pltpu.roll(part, k, 1)
        return near, far

    near, far = lax.fori_loop(
        0, rows - 2 * HALO, to_profile,
        (jnp.zeros((chans, LANES), jnp.float32), jnp.zeros((chans, 2 * LANES), jnp.float32)),
    )
    near = far[:, :LANES] + near
    zero = jnp.zeros((chans, LANES), jnp.float32)
    whole = jnp.concatenate([near, far[:, LANES:], zero], axis=1)
    corner = first + LANES
    tile = corner // LANES
    whole = pltpu.roll(whole, lax.rem(corner, LANES), 1)
    for b in range(gpad.shape[0]):
        gpad[b] = zero
    for b in range(3):
        gpad[tile + b] = whole[:, b * LANES : (b + 1) * LANES]

    rows_trans = tcot.shape[1]
    row_start = pl.multiple_of((chan_pos * 2 + sub_pos) * rows_trans, 8)
    for n in range(tcot.shape[0]):
        p, q = pairs[n, 0], pairs[n, 1]
        first_rows = prof[pl.ds(pl.multiple_of(p * LANES + row_start, 8), rows_trans), :] * ro_row[...]
        second = prof[pl.ds(pl.multiple_of(q * LANES, 8), LANES), :]
        row_pos = p * LANES + row_start + lax.broadcasted_iota(jnp.int32, (rows_trans, LANES), 0)
        col_pos = q * LANES + lax.broadcasted_iota(jnp.int32, (rows_trans, LANES), 1)
        cross = (end_of(row_pos) != end_of(col_pos)).astype(jnp.float32)
        maps[n] = mm(first_rows, second, NT, EXACT) * cross
        spent[...] = jnp.zeros_like(spent)
        spent[pl.ds(row_start, rows_trans), :] = tcot[n] * cross
        to_first = mm(prof_t[q], spent[...], NT, EXACT) * ro
        to_second = mm(prof_t[p] * ro, spent[...], NN, EXACT)
        gpad[1 + p] = gpad[1 + p] + to_first
        gpad[1 + q] = gpad[1 + q] + to_second

    pieces = []
    for b in range(seq_count):
        part[b] = gpad[1 + b].astype(jnp.bfloat16)
        pieces.append(split(gpad[1 + b]))
    for c in range(chan_count):
        total_proj = jnp.zeros((chans, width), jnp.float32)
        for b in range(seq_count):
            block = feats[c, (b + 1) * LANES : (b + 2) * LANES, :]
            total_proj = total_proj + mm(pieces[b][0], block) + mm(pieces[b][1], block)
        blank = jnp.zeros((chans, LANES - width), jnp.float32)
        misc[c] = (rest[c] + jnp.concatenate([total_proj, blank], axis=1)).astype(jnp.bfloat16)


def per_device(
    features, proj, kernel, mix, readout, dilations, chrom_lengths, pairs, contact_cot, trans_cot
):
    f32, bf16 = jnp.float32, jnp.bfloat16
    bin_dev, width = features.shape
    chans = proj.shape[1]
    band_dev = contact_cot.shape[0]
    layers, chan_dev = kernel.shape[:2]
    seq_count, chan_count = lax.axis_size("seq"), lax.axis_size("chan")
    total = bin_dev * seq_count
    rows = band_dev + 3 * HALO
    smem = pl.BlockSpec(memory_space=pltpu.SMEM)
    vmem = pl.BlockSpec(memory_space=pltpu.VMEM)
    shape = jax.ShapeDtypeStruct
    proj_t = proj.T

    def sems(count):
        return [pltpu.SemaphoreType.DMA((count,))] * 2

    gathered = pl.pallas_call(
        gather_kernel,
        out_shape=(
            shape((chan_count, (seq_count + 3) * bin_dev, width), bf16),
            shape((chan_count, chans, width), bf16),
            shape((chan_count, layers, chans, chan_dev), bf16),
            shape((chan_count, layers, chan_dev, 9), f32),
            shape((HALO, bin_dev), f32),
            shape((band_dev, bin_dev), f32),
            shape((HALO, bin_dev), f32),
        ),
        in_specs=[vmem] * 5,
        out_specs=(vmem,) * 7,
        scratch_shapes=[
            *sems(seq_count * chan_count - 1), *sems(3 * (chan_count - 1)), *sems(3)
        ],
        compiler_params=pltpu.CompilerParams(collective_id=0, has_side_effects=True),
    )(features, proj_t, mix, kernel, contact_cot)
    feats, projs, mixes, taps, edge, side, side_edge = gathered

    field = pltpu.VMEM((2 * LOW + rows, chans, LANES), f32)
    plain = pltpu.VMEM((rows, chans, LANES), f32)
    wide = BATCH * chans
    contact, maps, part, misc = pl.pallas_call(
        band_kernel,
        out_shape=(
            shape((band_dev, LANES), f32),
            shape(trans_cot.shape, f32),
            shape((seq_count, chans, LANES), bf16),
            shape((chan_count, chans, LANES), bf16),
        ),
        in_specs=[smem] * 3 + [vmem] * 11,
        out_specs=(vmem,) * 4,
        scratch_shapes=[
            pltpu.VMEM((layers, 9, chans, LANES), f32),
            pltpu.VMEM((2 * layers, wide, wide), bf16),
            pltpu.VMEM((chans, 2 * LANES), f32),
            pltpu.VMEM((total, chans), f32),
            pltpu.VMEM((seq_count, chans, LANES), f32),
            field,
            field,
            pltpu.VMEM((layers, rows, chans, LANES), bf16),
            plain,
            field,
            plain,
            plain,
            field,
            pltpu.VMEM((seq_count + 3, chans, LANES), f32),
            pltpu.VMEM((wide, wide), f32),
            pltpu.VMEM((LANES, LANES), f32),
            pltpu.VMEM((band_dev + HALO, LANES), f32),
            pltpu.VMEM((band_dev + HALO, LANES), f32),
            pltpu.VMEM((chan_count, chans, LANES), f32),
        ],
        compiler_params=pltpu.CompilerParams(vmem_limit_bytes=48 * 1024 * 1024),
    )(
        dilations, chrom_lengths, pairs, feats, projs, mixes, taps,
        readout[:, None], readout[None, :], contact_cot, edge, side, side_edge, trans_cot,
    )
    contact, grad_features, grad_proj, grad_kernel, grad_mix = pl.pallas_call(
        reduce_kernel,
        out_shape=(
            shape((band_dev, LANES), f32),
            shape((bin_dev, width), f32),
            shape((width, chans), f32),
            shape((layers, chan_dev, 9), f32),
            shape((layers, chans, chan_dev), f32),
        ),
        in_specs=[vmem] * 4,
        out_specs=(vmem,) * 5,
        scratch_shapes=[
            pltpu.VMEM((seq_count, chans, LANES), bf16),
            pltpu.VMEM((seq_count, chan_count, chans, LANES), bf16),
            pltpu.VMEM((chan_count, band_dev, LANES), f32),
            pltpu.VMEM((chan_count, 2, chans, LANES), f32),
            pltpu.VMEM((2 * chan_count, 2, chans, LANES), f32),
            pltpu.VMEM((chans, LANES), f32),
            *sems(2 * (seq_count - 1)), *sems(2 * chan_count - 1), *sems(chan_count - 1),
        ],
        compiler_params=pltpu.CompilerParams(collective_id=1, has_side_effects=True),
    )(part, misc, contact, proj_t)
    return (contact, maps, grad_features, grad_proj, grad_kernel, grad_mix)


def solution(mesh):
    in_specs = (
        P(("groups", "seq"), "chan"),
        P("chan", None),
        P(None, "chan", None),
        P(None, None, "chan"),
        P(),
        P(),
        P(),
        P(("groups", "seq"), None),
        P("sub", ("groups", "seq")),
        P(("groups", "seq"), ("chan", "sub"), None),
    )
    out_specs = (
        P("sub", ("groups", "seq")),
        P(("groups", "seq"), ("chan", "sub"), None),
        P(("groups", "seq"), "chan"),
        P(("groups", "chan"), None),
        P("groups", "chan", None),
        P("groups", None, "chan"),
    )
    return jax.shard_map(
        per_device, mesh=mesh, in_specs=in_specs, out_specs=out_specs, check_vma=False
    )
```

```python
import jax
import jax.numpy as jnp
from jax import lax
from jax.experimental import pallas as pl
from jax.experimental.pallas import tpu as pltpu
from jax.sharding import PartitionSpec as P

HALO = 8
LANES = 128
GUARD = 32
LOW = 16
BATCH = 8
MESH = pl.DeviceIdType.MESH
EXACT = lax.Precision.HIGHEST
NT = (((1,), (1,)), ((), ()))
NN = (((1,), (0,)), ((), ()))


def mm(a, b, dims=NN, precision=None):
    return lax.dot_general(a, b, dims, precision=precision, preferred_element_type=jnp.float32)


def split(value):
    high = value.astype(jnp.bfloat16)
    return high, (value - high.astype(jnp.float32)).astype(jnp.bfloat16)


def place():
    return lax.axis_index("seq"), lax.axis_index("chan"), lax.axis_index("sub")


def meet(sources, target_count):
    barrier = pltpu.get_barrier_semaphore()
    for device in sources:
        pl.semaphore_signal(barrier, inc=1, device_id=device, device_id_type=MESH)
    pl.semaphore_wait(barrier, target_count)


def at(s, x, u):
    return {"seq": s, "chan": x, "sub": u}


def gather_kernel(
    features, proj_t, mix, taps, cot,
    feats, projs, mixes, taps_all, edge, side, side_edge,
    send_feats, recv_feats, send_small, recv_small, send_cot, recv_cot,
):
    seq_count, chan_count = lax.axis_size("seq"), lax.axis_size("chan")
    s, x, u = place()
    band = cot.shape[0]
    peers, sources = [], []
    for ds in range(seq_count):
        for dx in range(chan_count):
            if ds or dx:
                peers.append(at(lax.rem(s + ds, seq_count), lax.rem(x + dx, chan_count), u))
                back = (lax.rem(s + seq_count - ds, seq_count), lax.rem(x + chan_count - dx, chan_count))
                sources.append(at(*back, u))
    step = jnp.where(x == 0, 1, seq_count - 1)
    ahead = lax.rem(s + step, seq_count)
    behind = lax.rem(s + seq_count - step, seq_count)
    other = 1 - u
    meet(sources + [at(s, x, other), at(behind, x, other)], len(peers) + 2)

    copies = []

    def push(source, target, sems, j, device):
        copy = pltpu.make_async_remote_copy(
            src_ref=source, dst_ref=target, send_sem=sems[0].at[j], recv_sem=sems[1].at[j],
            device_id=device, device_id_type=MESH,
        )
        copy.start()
        copies.append(copy)

    rim = pl.ds(pl.multiple_of((1 - u) * (band - HALO), HALO), HALO)
    for j, device in enumerate(peers):
        push(features, feats.at[x, s], (send_feats, recv_feats), j, device)
    push(cot, side, (send_cot, recv_cot), 0, at(ahead, x, u))
    push(cot.at[rim], side_edge, (send_cot, recv_cot), 1, at(ahead, x, other))
    push(cot.at[rim], edge, (send_cot, recv_cot), 2, at(s, x, other))
    for dx in range(1, chan_count):
        device = at(s, lax.rem(x + dx, chan_count), u)
        small = (send_small, recv_small)
        push(proj_t, projs.at[x], small, 3 * dx - 3, device)
        push(mix, mixes.at[x], small, 3 * dx - 2, device)
        push(taps, taps_all.at[x], small, 3 * dx - 1, device)
    feats[x, s] = features[...]
    projs[x] = proj_t[...]
    mixes[x] = mix[...]
    taps_all[x] = taps[...]
    for copy in copies:
        copy.wait()


def reduce_kernel(
    part, misc, contact, proj_t,
    contact_out, grad_features, grad_proj, grad_kernel, grad_mix,
    parts, miscs, contacts, outgoing, arrived, taps_sum, send_a, recv_a, send_b, recv_b, send_c, recv_c,
):
    seq_count, chan_count = lax.axis_size("seq"), lax.axis_size("chan")
    s, x, u = place()
    layers, chan_dev = grad_kernel.shape[0], grad_kernel.shape[1]
    chans, width = proj_t.shape
    far = [lax.rem(s + j, seq_count) for j in range(1, seq_count)]
    near = [(dx, du) for dx in range(chan_count) for du in range(2) if dx or du]

    def neighbour(dx, du):
        return lax.rem(x + dx, chan_count), lax.rem(u + du, 2)

    everyone = [at(t, x, u) for t in far] + [at(s, *neighbour(dx, du)) for dx, du in near]
    meet(everyone, len(everyone))
    copies = []

    def push(source, target, sems, j, device):
        copy = pltpu.make_async_remote_copy(
            src_ref=source, dst_ref=target, send_sem=sems[0].at[j], recv_sem=sems[1].at[j],
            device_id=device, device_id_type=MESH,
        )
        copy.start()
        return copy

    first = []
    for j, t in enumerate(far):
        first.append(push(misc, miscs.at[s], (send_a, recv_a), 2 * j, at(t, x, u)))
        first.append(push(part.at[t], parts.at[s], (send_a, recv_a), 2 * j + 1, at(t, x, u)))
    shown = []
    for dx in range(1, chan_count):
        device = at(s, lax.rem(x + dx, chan_count), u)
        shown.append(push(contact, contacts.at[x], (send_c, recv_c), dx - 1, device))
    parts[s] = part[s]
    miscs[s] = misc[...]
    contacts[x] = contact[...]
    for copy in first:
        copy.wait()
    f32 = jnp.float32
    total = parts[0].astype(f32)
    for t in range(1, seq_count):
        total = total + parts[t].astype(f32)
    for c in range(chan_count):
        outgoing[c, 0] = total
        rest = miscs[0, c].astype(f32)
        for t in range(1, seq_count):
            rest = rest + miscs[t, c].astype(f32)
        outgoing[c, 1] = rest
    second = []
    for j, (dx, du) in enumerate(near):
        nx, nu = neighbour(dx, du)
        second.append(
            push(outgoing.at[nx], arrived.at[2 * x + u], (send_b, recv_b), j, at(s, nx, nu))
        )
    arrived[2 * x + u] = outgoing[x]
    for copy in shown:
        copy.wait()
    picture = contacts[0]
    for c in range(1, chan_count):
        picture = picture + contacts[c]
    contact_out[...] = picture
    for copy in second:
        copy.wait()
    total, rest = arrived[0, 0], arrived[0, 1]
    for j in range(1, 2 * chan_count):
        total, rest = total + arrived[j, 0], rest + arrived[j, 1]
    blank = jnp.zeros((chans, LANES - width), f32)
    proj = jnp.concatenate([proj_t[...].astype(f32), blank], axis=1).T[:width]
    grad_features[...] = mm(proj, total, NN, EXACT)
    grad_proj[...] = rest[:, :width]
    flipped = rest.T
    for l in range(layers):
        grad_mix[l] = flipped[width + l * chan_dev : width + (l + 1) * chan_dev]
        off = width + layers * chan_dev + 9 * l
        taps_sum[...] = rest
        grad_kernel[l] = taps_sum[pl.ds(x * chan_dev, chan_dev), off : off + 9]


def band_kernel(
    dil, chroms, pairs, feats, projs, mixes, taps_in, ro_col, ro_row,
    cot_own, cot_edge, cot_side, cot_side_edge, tcot,
    contact, maps, part, misc,
    taps, spread, env, prof, prof_t, x0, x1, h, go, gs, gf, go1, gs1, gpad, acc, spent, cot, picture, rest, mixed_t,
):
    chans, width = projs.shape[1:]
    layers, chan_dev = mixes.shape[1], mixes.shape[2]
    bin_dev = LANES
    seq_count, chan_count = lax.axis_size("seq"), lax.axis_size("chan")
    seq_pos, chan_pos, sub_pos = place()
    total = seq_count * bin_dev
    own_bins = bin_dev // chan_count
    rows = h.shape[1]
    own_rows = rows - 3 * HALO
    wide = BATCH * chans
    first = seq_pos * bin_dev + chan_pos * own_bins - GUARD
    k_base = sub_pos * (own_rows - 3 * HALO)
    own_start = sub_pos * 3 * HALO
    is_low = (sub_pos == 0).astype(jnp.float32)

    ends, run = [], jnp.int32(0)
    for j in range(chroms.shape[0]):
        run = run + chroms[j]
        ends.append(run)

    def end_of(pos):
        best = jnp.full(pos.shape, 1 << 20, jnp.int32)
        for e in ends:
            best = jnp.minimum(best, jnp.where(pos < e, e, 1 << 20))
        return best

    pos = first + lax.broadcasted_iota(jnp.int32, (1, LANES), 1)
    left = jnp.where((pos >= 0) & (pos < total), end_of(pos) - pos, 0)
    lane = lax.broadcasted_iota(jnp.int32, (1, LANES), 1)
    own_lane = ((lane >= GUARD) & (lane < GUARD + own_bins)).astype(jnp.float32)

    def mask(r):
        return (k_base + r < left).astype(jnp.float32)

    r_i = lax.broadcasted_iota(jnp.int32, (wide, chans), 0)
    c_i = lax.broadcasted_iota(jnp.int32, (wide, chans), 1)
    fan = (lax.rem(r_i, chans) == c_i).astype(jnp.bfloat16)
    r_w = lax.broadcasted_iota(jnp.int32, (wide, wide), 0) // chans
    c_w = lax.broadcasted_iota(jnp.int32, (wide, wide), 1) // chans
    diag = r_w == c_w
    for l in range(layers):
        for c in range(chan_count):
            mixed_t[c * chan_dev : (c + 1) * chan_dev, :] = mixes[c, l].astype(jnp.float32)
        mixed = mixed_t[...].astype(jnp.bfloat16)
        for side, dims in enumerate((NN, NT)):
            tall = mm(fan, mixed, dims).astype(jnp.bfloat16)
            full = mm(tall, fan, NT)
            spread[2 * l + side] = jnp.where(diag, full, 0.0).astype(jnp.bfloat16)
        for t in range(9):
            for c in range(chan_count):
                column = taps_in[c, l][:, t : t + 1]
                taps[l, t, c * chan_dev : (c + 1) * chan_dev, :] = jnp.broadcast_to(
                    column, (chan_dev, LANES)
                )

    turn = lax.rem(LANES + GUARD - chan_pos * own_bins, LANES)
    column = lane - GUARD + chan_pos * own_bins
    inside = (column >= 0) & (column < LANES)
    own_at = pl.multiple_of(sub_pos * HALO, HALO)
    lines = [
        jnp.where(inside, pltpu.roll(here[...], turn, 1), pltpu.roll(there[...], turn, 1))
        for here, there in ((cot_own, cot_side), (cot_edge, cot_side_edge))
    ]
    cot[...] = jnp.where(
        sub_pos == 0,
        jnp.concatenate(lines, axis=0),
        jnp.concatenate(lines[::-1], axis=0),
    )

    zero = jnp.zeros((chans, LANES), jnp.float32)
    for b in (0, seq_count + 1, seq_count + 2):
        prof_t[b] = zero
    for b in range(seq_count):
        sums = [mm(projs[c], feats[c, b]) for c in range(chan_count)]
        block = sum(sums[1:], sums[0])
        prof_t[1 + b] = block
        prof[b * LANES : (b + 1) * LANES, :] = block.T
    corner = first + LANES
    tile, lead = corner // LANES, lax.rem(corner, LANES)
    around = jnp.concatenate([prof_t[tile], prof_t[tile + 1], prof_t[tile + 2]], axis=1)
    env[...] = pltpu.roll(around, lax.rem(3 * LANES - lead, 3 * LANES), 1)[:, : 2 * LANES]
    ro = jnp.broadcast_to(ro_col[...], (chans, LANES))

    for buf in (x0, x1, gs, gs1):
        for r in (*range(LOW), *range(LOW + rows, 2 * LOW + rows)):
            buf[r] = jnp.zeros((chans, LANES), jnp.float32)

    def clear(i, _):
        gs[LOW + i] = jnp.zeros((chans, LANES), jnp.float32)
        gs1[LOW + i] = jnp.zeros((chans, LANES), jnp.float32)
        go1[i] = jnp.zeros((chans, LANES), jnp.float32)
        return 0

    lax.fori_loop(0, rows, clear, 0, unroll=4)

    def build(i, _):
        k = k_base + i
        moved = pltpu.roll(env[...], lax.rem(2 * LANES - k, 2 * LANES), 1)[:, :LANES]
        x0[LOW + i] = env[:, :LANES] * moved * mask(i)
        return 0

    lax.fori_loop(0, rows, build, 0, unroll=4)

    def conv(x, l, d, r, sign):
        lines = [x[LOW + r + sign * b * d] for b in (-1, 0, 1)]
        sums = []
        for a in range(3):
            t = [taps[l, 3 * a + b] * lines[b] for b in range(3)]
            sums.append(t[0] + t[1] + t[2])
        fwd, back = (d, LANES - d) if sign > 0 else (LANES - d, d)
        return sums[1] + pltpu.roll(sums[0], fwd, 1) + pltpu.roll(sums[2], back, 1)

    xs = [x0, x1]
    for l in range(layers):
        d = dil[l]
        x = xs[l]
        for m in range(1, HALO + 1):
            x[LOW - m] = x[LOW + m]
        base = sub_pos * HALO * (l + 1)

        def layer(i, _, l=l, d=d, x=x, base=base):
            r0 = base + i * BATCH
            for j in range(BATCH):
                summed = conv(x, l, d, r0 + j, 1)
                h[l, r0 + j] = jnp.maximum(summed, 0.0).astype(jnp.bfloat16)
            upd = mm(spread[2 * l], h[l, pl.ds(r0, BATCH)].reshape(wide, LANES))
            upd = upd.reshape(BATCH, chans, LANES)
            for j in range(BATCH):
                new = (x[LOW + r0 + j] + upd[j]) * mask(r0 + j)
                if l + 1 < layers:
                    xs[l + 1][LOW + r0 + j] = new
                else:
                    picture[pl.ds(i * BATCH + j, 1), :] = jnp.sum(new * ro, axis=0, keepdims=True)
            return 0

        lax.fori_loop(0, (rows - HALO * (l + 1)) // BATCH, layer, 0)

    shown = picture[pl.ds(own_at, own_rows), :] * own_lane
    contact[...] = pltpu.roll(shown, lax.rem(LANES - turn, LANES), 1)
    for c in range(chan_count):
        rest[c] = jnp.zeros((chans, LANES), jnp.float32)

    def pull(l, r0, source, target):
        g = source[pl.ds(r0, BATCH)].reshape(wide, LANES)
        high, low = split(g)
        gh = mm(spread[2 * l + 1], high) + mm(spread[2 * l + 1], low)
        gh = gh.astype(jnp.bfloat16).astype(jnp.float32).reshape(BATCH, chans, LANES)
        for j in range(BATCH):
            on = h[l, r0 + j].astype(jnp.float32) > 0
            target[LOW + r0 + j] = jnp.where(on, gh[j], 0.0)

    def weight_grads(l, x, d, g_out, g_sum):
        acc[...] = jnp.zeros_like(acc)

        def body(i, sums):
            r0 = own_start + i * BATCH
            g = (g_out[pl.ds(r0, BATCH)] * own_lane).astype(jnp.bfloat16).reshape(wide, LANES)
            acc[...] += mm(h[l, pl.ds(r0, BATCH)].reshape(wide, LANES), g, NT)
            for j in range(BATCH):
                r = r0 + j
                g0 = g_sum[LOW + r] * own_lane
                moved = (pltpu.roll(g0, LANES - d, 1), g0, pltpu.roll(g0, d, 1))
                lines = [x[LOW + r + b * d] for b in (-1, 0, 1)]
                sums = tuple(sums[t] + moved[t // 3] * lines[t % 3] for t in range(9))
            return sums

        zero = jnp.zeros((chans, LANES), jnp.float32)
        sums = lax.fori_loop(0, own_rows // BATCH, body, (zero,) * 9)
        tile = jnp.zeros((chans, LANES), jnp.float32)
        for t in range(9):
            line = jnp.sum(sums[t], axis=1, keepdims=True)
            off = width + layers * chan_dev + 9 * l + t
            tile = tile + jnp.where(lane == off, line, 0.0)
        tall = jnp.sum(jnp.where(diag, acc[...], 0.0).reshape(BATCH, chans, wide), axis=0)
        row_e = lax.rem(lax.broadcasted_iota(jnp.int32, (wide, LANES), 0), chans)
        col_e = lax.broadcasted_iota(jnp.int32, (wide, LANES), 1) - width - l * chan_dev
        for c in range(chan_count):
            hit = (col_e >= 0) & (col_e < chan_dev) & (row_e == col_e + c * chan_dev)
            rest[c] = rest[c] + tile + mm(tall, hit.astype(jnp.float32), precision=EXACT)

    def last_out(i, _):
        r0 = sub_pos * 2 * HALO + i * BATCH
        for j in range(BATCH):
            line = cot[pl.ds(i * BATCH + j, 1), :] * mask(r0 + j)
            go[r0 + j] = ro * line
        pull(1, r0, go, gs)
        return 0

    lax.fori_loop(0, (rows - 2 * HALO) // BATCH, last_out, 0)
    weight_grads(1, x1, dil[1], go, gs)

    def fold(l, d, g, target):
        for m in range(1, HALO + 1):
            target[m] = target[m] + is_low * conv(g, l, d, -m, -1)

    def back_field(i, _):
        r0 = own_start + i * BATCH
        for j in range(BATCH):
            gf[r0 + j] = go[r0 + j] + conv(gs, 1, dil[1], r0 + j, -1)
        return 0

    lax.fori_loop(0, own_rows // BATCH, back_field, 0)
    fold(1, dil[1], gs, gf)

    def first_out(i, _):
        r0 = own_start + i * BATCH
        for j in range(BATCH):
            go1[r0 + j] = gf[r0 + j] * (mask(r0 + j) * own_lane)
        pull(0, r0, go1, gs1)
        return 0

    lax.fori_loop(0, own_rows // BATCH, first_out, 0)
    weight_grads(0, x0, dil[0], go1, gs1)

    def back_first(i, _):
        r0 = sub_pos * 2 * HALO + i * BATCH
        for j in range(BATCH):
            gf[r0 + j] = go1[r0 + j] + conv(gs1, 0, dil[0], r0 + j, -1)
        return 0

    lax.fori_loop(0, (rows - 2 * HALO) // BATCH, back_first, 0)
    fold(0, dil[0], gs1, gf)

    def to_profile(i, carry):
        near, far = carry
        r = sub_pos * 2 * HALO + i
        k = k_base + r
        g = gf[r] * mask(r)
        moved = pltpu.roll(env[...], lax.rem(2 * LANES - k, 2 * LANES), 1)[:, :LANES]
        near = near + g * moved
        part = jnp.concatenate([g * env[:, :LANES], jnp.zeros((chans, LANES), jnp.float32)], axis=1)
        far = far + pltpu.roll(part, k, 1)
        return near, far

    near, far = lax.fori_loop(
        0, rows - 2 * HALO, to_profile,
        (jnp.zeros((chans, LANES), jnp.float32), jnp.zeros((chans, 2 * LANES), jnp.float32)),
    )
    near = far[:, :LANES] + near
    whole = jnp.concatenate([near, far[:, LANES:], zero], axis=1)
    whole = pltpu.roll(whole, lead, 1)
    for b in range(gpad.shape[0]):
        gpad[b] = zero
    for b in range(3):
        gpad[tile + b] = whole[:, b * LANES : (b + 1) * LANES]

    rows_trans = tcot.shape[1]
    row_start = pl.multiple_of((chan_pos * 2 + sub_pos) * rows_trans, 8)
    for n in range(tcot.shape[0]):
        p, q = pairs[n, 0], pairs[n, 1]
        first_rows = prof[pl.ds(pl.multiple_of(p * LANES + row_start, 8), rows_trans), :] * ro_row[...]
        row_pos = p * LANES + row_start + lax.broadcasted_iota(jnp.int32, (rows_trans, LANES), 0)
        col_pos = q * LANES + lax.broadcasted_iota(jnp.int32, (rows_trans, LANES), 1)
        cross = (end_of(row_pos) != end_of(col_pos)).astype(jnp.float32)
        maps[n] = mm(first_rows, prof_t[1 + q], NN, EXACT) * cross
        spent[...] = jnp.zeros_like(spent)
        spent[pl.ds(row_start, rows_trans), :] = tcot[n] * cross
        to_first = mm(prof_t[1 + q], spent[...], NT, EXACT) * ro
        to_second = mm(prof_t[1 + p] * ro, spent[...], NN, EXACT)
        gpad[1 + p] = gpad[1 + p] + to_first
        gpad[1 + q] = gpad[1 + q] + to_second

    pieces = []
    for b in range(seq_count):
        part[b] = gpad[1 + b].astype(jnp.bfloat16)
        pieces.append(split(gpad[1 + b]))
    for c in range(chan_count):
        total_proj = jnp.zeros((chans, width), jnp.float32)
        for b in range(seq_count):
            block = feats[c, b]
            total_proj = total_proj + mm(pieces[b][0], block, NT) + mm(pieces[b][1], block, NT)
        blank = jnp.zeros((chans, LANES - width), jnp.float32)
        misc[c] = (rest[c] + jnp.concatenate([total_proj, blank], axis=1)).astype(jnp.bfloat16)


def per_device(
    features, proj, kernel, mix, readout, dilations, chrom_lengths, pairs, contact_cot, trans_cot
):
    f32, bf16 = jnp.float32, jnp.bfloat16
    bin_dev, width = features.shape
    chans = proj.shape[1]
    band_dev = contact_cot.shape[0]
    layers, chan_dev = kernel.shape[:2]
    seq_count, chan_count = lax.axis_size("seq"), lax.axis_size("chan")
    total = bin_dev * seq_count
    rows = band_dev + 3 * HALO
    smem = pl.BlockSpec(memory_space=pltpu.SMEM)
    vmem = pl.BlockSpec(memory_space=pltpu.VMEM)
    shape = jax.ShapeDtypeStruct
    proj_t = proj.T

    def sems(count):
        return [pltpu.SemaphoreType.DMA((count,))] * 2

    gathered = pl.pallas_call(
        gather_kernel,
        out_shape=(
            shape((chan_count, seq_count, width, bin_dev), bf16),
            shape((chan_count, chans, width), bf16),
            shape((chan_count, layers, chan_dev, chans), bf16),
            shape((chan_count, layers, chan_dev, 9), f32),
            shape((HALO, bin_dev), f32),
            shape((band_dev, bin_dev), f32),
            shape((HALO, bin_dev), f32),
        ),
        in_specs=[vmem] * 5,
        out_specs=(vmem,) * 7,
        scratch_shapes=[
            *sems(seq_count * chan_count - 1), *sems(3 * (chan_count - 1)), *sems(3)
        ],
        compiler_params=pltpu.CompilerParams(collective_id=0, has_side_effects=True),
    )(features.T, proj_t, mix.transpose(0, 2, 1), kernel, contact_cot)
    feats, projs, mixes, taps, edge, side, side_edge = gathered

    field = pltpu.VMEM((2 * LOW + rows, chans, LANES), f32)
    plain = pltpu.VMEM((rows, chans, LANES), f32)
    wide = BATCH * chans
    contact, maps, part, misc = pl.pallas_call(
        band_kernel,
        out_shape=(
            shape((band_dev, LANES), f32),
            shape(trans_cot.shape, f32),
            shape((seq_count, chans, LANES), bf16),
            shape((chan_count, chans, LANES), bf16),
        ),
        in_specs=[smem] * 3 + [vmem] * 11,
        out_specs=(vmem,) * 4,
        scratch_shapes=[
            pltpu.VMEM((layers, 9, chans, LANES), f32),
            pltpu.VMEM((2 * layers, wide, wide), bf16),
            pltpu.VMEM((chans, 2 * LANES), f32),
            pltpu.VMEM((total, chans), f32),
            pltpu.VMEM((seq_count + 3, chans, LANES), f32),
            field,
            field,
            pltpu.VMEM((layers, rows, chans, LANES), bf16),
            plain,
            field,
            plain,
            plain,
            field,
            pltpu.VMEM((seq_count + 3, chans, LANES), f32),
            pltpu.VMEM((wide, wide), f32),
            pltpu.VMEM((LANES, LANES), f32),
            pltpu.VMEM((band_dev + HALO, LANES), f32),
            pltpu.VMEM((band_dev + HALO, LANES), f32),
            pltpu.VMEM((chan_count, chans, LANES), f32),
            pltpu.VMEM((chans, chans), f32),
        ],
        compiler_params=pltpu.CompilerParams(vmem_limit_bytes=48 * 1024 * 1024),
    )(
        dilations, chrom_lengths, pairs, feats, projs, mixes, taps,
        readout[:, None], readout[None, :], contact_cot, edge, side, side_edge, trans_cot,
    )
    contact, grad_features, grad_proj, grad_kernel, grad_mix = pl.pallas_call(
        reduce_kernel,
        out_shape=(
            shape((band_dev, LANES), f32),
            shape((width, bin_dev), f32),
            shape((chans, width), f32),
            shape((layers, chan_dev, 9), f32),
            shape((layers, chan_dev, chans), f32),
        ),
        in_specs=[vmem] * 4,
        out_specs=(vmem,) * 5,
        scratch_shapes=[
            pltpu.VMEM((seq_count, chans, LANES), bf16),
            pltpu.VMEM((seq_count, chan_count, chans, LANES), bf16),
            pltpu.VMEM((chan_count, band_dev, LANES), f32),
            pltpu.VMEM((chan_count, 2, chans, LANES), f32),
            pltpu.VMEM((2 * chan_count, 2, chans, LANES), f32),
            pltpu.VMEM((chans, LANES), f32),
            *sems(2 * (seq_count - 1)), *sems(2 * chan_count - 1), *sems(chan_count - 1),
        ],
        compiler_params=pltpu.CompilerParams(collective_id=1, has_side_effects=True),
    )(part, misc, contact, proj_t)
    return (contact, maps, grad_features.T, grad_proj.T, grad_kernel, grad_mix.transpose(0, 2, 1))


def solution(mesh):
    in_specs = (
        P(("groups", "seq"), "chan"),
        P("chan", None),
        P(None, "chan", None),
        P(None, None, "chan"),
        P(),
        P(),
        P(),
        P(("groups", "seq"), None),
        P("sub", ("groups", "seq")),
        P(("groups", "seq"), ("chan", "sub"), None),
    )
    out_specs = (
        P("sub", ("groups", "seq")),
        P(("groups", "seq"), ("chan", "sub"), None),
        P(("groups", "seq"), "chan"),
        P(("groups", "chan"), None),
        P("groups", "chan", None),
        P("groups", None, "chan"),
    )
    return jax.shard_map(
        per_device, mesh=mesh, in_specs=in_specs, out_specs=out_specs, check_vma=False
    )
```

```python
import jax
import jax.numpy as jnp
from jax import lax
from jax.experimental import pallas as pl
from jax.experimental.pallas import tpu as pltpu
from jax.sharding import PartitionSpec as P

HALO = 8
LANES = 128
GUARD = 32
LOW = 16
BATCH = 8
MESH = pl.DeviceIdType.MESH
EXACT = lax.Precision.HIGHEST
NT = (((1,), (1,)), ((), ()))
NN = (((1,), (0,)), ((), ()))


def mm(a, b, dims=NN, precision=None):
    return lax.dot_general(a, b, dims, precision=precision, preferred_element_type=jnp.float32)


def split(value):
    high = value.astype(jnp.bfloat16)
    return high, (value - high.astype(jnp.float32)).astype(jnp.bfloat16)


def place():
    return lax.axis_index("seq"), lax.axis_index("chan"), lax.axis_index("sub")


def meet(sources, target_count):
    barrier = pltpu.get_barrier_semaphore()
    for device in sources:
        pl.semaphore_signal(barrier, inc=1, device_id=device, device_id_type=MESH)
    pl.semaphore_wait(barrier, target_count)


def at(s, x, u):
    return {"seq": s, "chan": x, "sub": u}


def gather_kernel(
    features, proj_t, mix, taps, cot,
    feats, projs, mixes, taps_all, edge, side, side_edge,
    send_feats, recv_feats, send_small, recv_small, send_cot, recv_cot,
):
    seq_count, chan_count = lax.axis_size("seq"), lax.axis_size("chan")
    s, x, u = place()
    band = cot.shape[0]
    peers, sources = [], []
    for ds in range(seq_count):
        for dx in range(chan_count):
            if ds or dx:
                peers.append(at(lax.rem(s + ds, seq_count), lax.rem(x + dx, chan_count), u))
                back = (lax.rem(s + seq_count - ds, seq_count), lax.rem(x + chan_count - dx, chan_count))
                sources.append(at(*back, u))
    step = jnp.where(x == 0, 1, seq_count - 1)
    ahead = lax.rem(s + step, seq_count)
    behind = lax.rem(s + seq_count - step, seq_count)
    other = 1 - u
    meet(sources + [at(s, x, other), at(behind, x, other)], len(peers) + 2)

    copies = []

    def push(source, target, sems, j, device):
        copy = pltpu.make_async_remote_copy(
            src_ref=source, dst_ref=target, send_sem=sems[0].at[j], recv_sem=sems[1].at[j],
            device_id=device, device_id_type=MESH,
        )
        copy.start()
        copies.append(copy)

    rim = pl.ds(pl.multiple_of((1 - u) * (band - HALO), HALO), HALO)
    for j, device in enumerate(peers):
        push(features, feats.at[x, s], (send_feats, recv_feats), j, device)
    push(cot, side, (send_cot, recv_cot), 0, at(ahead, x, u))
    push(cot.at[rim], side_edge, (send_cot, recv_cot), 1, at(ahead, x, other))
    push(cot.at[rim], edge, (send_cot, recv_cot), 2, at(s, x, other))
    for dx in range(1, chan_count):
        device = at(s, lax.rem(x + dx, chan_count), u)
        small = (send_small, recv_small)
        push(proj_t, projs.at[x], small, 3 * dx - 3, device)
        push(mix, mixes.at[x], small, 3 * dx - 2, device)
        push(taps, taps_all.at[x], small, 3 * dx - 1, device)
    feats[x, s] = features[...]
    projs[x] = proj_t[...]
    mixes[x] = mix[...]
    taps_all[x] = taps[...]
    for copy in copies:
        copy.wait()


def reduce_kernel(
    part, misc, contact, proj_t,
    contact_out, grad_features, grad_proj, grad_kernel, grad_mix,
    parts, miscs, contacts, outgoing, arrived, taps_sum, send_a, recv_a, send_b, recv_b, send_c, recv_c,
):
    seq_count, chan_count = lax.axis_size("seq"), lax.axis_size("chan")
    s, x, u = place()
    layers, chan_dev = grad_kernel.shape[0], grad_kernel.shape[1]
    chans, width = proj_t.shape
    far = [lax.rem(s + j, seq_count) for j in range(1, seq_count)]
    near = [(dx, du) for dx in range(chan_count) for du in range(2) if dx or du]

    def neighbour(dx, du):
        return lax.rem(x + dx, chan_count), lax.rem(u + du, 2)

    everyone = [at(t, x, u) for t in far] + [at(s, *neighbour(dx, du)) for dx, du in near]
    meet(everyone, len(everyone))
    copies = []

    def push(source, target, sems, j, device):
        copy = pltpu.make_async_remote_copy(
            src_ref=source, dst_ref=target, send_sem=sems[0].at[j], recv_sem=sems[1].at[j],
            device_id=device, device_id_type=MESH,
        )
        copy.start()
        return copy

    first = []
    for j, t in enumerate(far):
        first.append(push(misc, miscs.at[s], (send_a, recv_a), 2 * j, at(t, x, u)))
        first.append(push(part.at[t], parts.at[s], (send_a, recv_a), 2 * j + 1, at(t, x, u)))
    shown = []
    for dx in range(1, chan_count):
        device = at(s, lax.rem(x + dx, chan_count), u)
        shown.append(push(contact, contacts.at[x], (send_c, recv_c), dx - 1, device))
    parts[s] = part[s]
    miscs[s] = misc[...]
    contacts[x] = contact[...]
    for copy in first:
        copy.wait()
    f32 = jnp.float32
    total = parts[0].astype(f32)
    for t in range(1, seq_count):
        total = total + parts[t].astype(f32)
    for c in range(chan_count):
        outgoing[c, 0] = total
        rest = miscs[0, c].astype(f32)
        for t in range(1, seq_count):
            rest = rest + miscs[t, c].astype(f32)
        outgoing[c, 1] = rest
    second = []
    for j, (dx, du) in enumerate(near):
        nx, nu = neighbour(dx, du)
        second.append(
            push(outgoing.at[nx], arrived.at[2 * x + u], (send_b, recv_b), j, at(s, nx, nu))
        )
    arrived[2 * x + u] = outgoing[x]
    for copy in shown:
        copy.wait()
    picture = contacts[0]
    for c in range(1, chan_count):
        picture = picture + contacts[c]
    contact_out[...] = picture
    for copy in second:
        copy.wait()
    total, rest = arrived[0, 0], arrived[0, 1]
    for j in range(1, 2 * chan_count):
        total, rest = total + arrived[j, 0], rest + arrived[j, 1]
    blank = jnp.zeros((chans, LANES - width), f32)
    proj = jnp.concatenate([proj_t[...].astype(f32), blank], axis=1).T[:width]
    grad_features[...] = mm(proj, total, NN, EXACT)
    grad_proj[...] = rest[:, :width]
    flipped = rest.T
    for l in range(layers):
        grad_mix[l] = flipped[width + l * chan_dev : width + (l + 1) * chan_dev]
        off = width + layers * chan_dev + 9 * l
        taps_sum[...] = rest
        grad_kernel[l] = taps_sum[pl.ds(x * chan_dev, chan_dev), off : off + 9]


def band_kernel(
    dil, chroms, pairs, feats, projs, mixes, taps_in, ro_col, ro_row,
    cot_own, cot_edge, cot_side, cot_side_edge, tcot,
    contact, maps, part, misc,
    taps, spread, env, prof, prof_t, x0, x1, h, go, gs, gf, go1, gs1, gpad, acc, spent, cot, picture, rest, mixed_t,
):
    chans, width = projs.shape[1:]
    layers, chan_dev = mixes.shape[1], mixes.shape[2]
    bin_dev = LANES
    seq_count, chan_count = lax.axis_size("seq"), lax.axis_size("chan")
    seq_pos, chan_pos, sub_pos = place()
    total = seq_count * bin_dev
    own_bins = bin_dev // chan_count
    rows = h.shape[1]
    own_rows = rows - 3 * HALO
    wide = BATCH * chans
    first = seq_pos * bin_dev + chan_pos * own_bins - GUARD
    k_base = sub_pos * (own_rows - 3 * HALO)
    own_start = sub_pos * 3 * HALO
    is_low = (sub_pos == 0).astype(jnp.float32)

    ends, run = [], jnp.int32(0)
    for j in range(chroms.shape[0]):
        run = run + chroms[j]
        ends.append(run)

    def end_of(pos):
        best = jnp.full(pos.shape, 1 << 20, jnp.int32)
        for e in ends:
            best = jnp.minimum(best, jnp.where(pos < e, e, 1 << 20))
        return best

    pos = first + lax.broadcasted_iota(jnp.int32, (1, LANES), 1)
    left = jnp.where((pos >= 0) & (pos < total), end_of(pos) - pos, 0)
    lane = lax.broadcasted_iota(jnp.int32, (1, LANES), 1)
    own_lane = ((lane >= GUARD) & (lane < GUARD + own_bins)).astype(jnp.float32)

    def mask(r):
        return (k_base + r < left).astype(jnp.float32)

    r_i = lax.broadcasted_iota(jnp.int32, (wide, chans), 0)
    c_i = lax.broadcasted_iota(jnp.int32, (wide, chans), 1)
    fan = (lax.rem(r_i, chans) == c_i).astype(jnp.bfloat16)
    r_w = lax.broadcasted_iota(jnp.int32, (wide, wide), 0) // chans
    c_w = lax.broadcasted_iota(jnp.int32, (wide, wide), 1) // chans
    diag = r_w == c_w
    for l in range(layers):
        for c in range(chan_count):
            mixed_t[c * chan_dev : (c + 1) * chan_dev, :] = mixes[c, l].astype(jnp.float32)
        mixed = mixed_t[...].astype(jnp.bfloat16)
        for side, dims in enumerate((NN, NT)):
            tall = mm(fan, mixed, dims).astype(jnp.bfloat16)
            full = mm(tall, fan, NT)
            spread[2 * l + side] = jnp.where(diag, full, 0.0).astype(jnp.bfloat16)
        for t in range(9):
            for c in range(chan_count):
                column = taps_in[c, l][:, t : t + 1]
                taps[l, t, c * chan_dev : (c + 1) * chan_dev, :] = jnp.broadcast_to(
                    column, (chan_dev, LANES)
                )

    turn = lax.rem(LANES + GUARD - chan_pos * own_bins, LANES)
    column = lane - GUARD + chan_pos * own_bins
    inside = (column >= 0) & (column < LANES)
    own_at = pl.multiple_of(sub_pos * HALO, HALO)
    lines = [
        jnp.where(inside, pltpu.roll(here[...], turn, 1), pltpu.roll(there[...], turn, 1))
        for here, there in ((cot_own, cot_side), (cot_edge, cot_side_edge))
    ]
    cot[...] = jnp.where(
        sub_pos == 0,
        jnp.concatenate(lines, axis=0),
        jnp.concatenate(lines[::-1], axis=0),
    )

    zero = jnp.zeros((chans, LANES), jnp.float32)
    for b in (0, seq_count + 1, seq_count + 2):
        prof_t[b] = zero
    for b in range(seq_count):
        sums = [mm(projs[c], feats[c, b]) for c in range(chan_count)]
        block = sum(sums[1:], sums[0])
        prof_t[1 + b] = block
        prof[b * LANES : (b + 1) * LANES, :] = block.T
    corner = first + LANES
    tile, lead = corner // LANES, lax.rem(corner, LANES)
    around = jnp.concatenate([prof_t[tile], prof_t[tile + 1], prof_t[tile + 2]], axis=1)
    env[...] = pltpu.roll(around, lax.rem(3 * LANES - lead, 3 * LANES), 1)[:, : 2 * LANES]
    ro = jnp.broadcast_to(ro_col[...], (chans, LANES))

    for buf in (x0, x1, gs, gs1):
        for r in (*range(LOW), *range(LOW + rows, 2 * LOW + rows)):
            buf[r] = jnp.zeros((chans, LANES), jnp.float32)

    def clear(i, _):
        gs[LOW + i] = jnp.zeros((chans, LANES), jnp.float32)
        gs1[LOW + i] = jnp.zeros((chans, LANES), jnp.float32)
        go1[i] = jnp.zeros((chans, LANES), jnp.float32)
        return 0

    lax.fori_loop(0, rows, clear, 0, unroll=4)

    def build(i, _):
        k = k_base + i
        moved = pltpu.roll(env[...], lax.rem(2 * LANES - k, 2 * LANES), 1)[:, :LANES]
        x0[LOW + i] = env[:, :LANES] * moved * mask(i)
        return 0

    lax.fori_loop(0, rows, build, 0, unroll=8)

    def conv(x, l, d, r, sign):
        lines = [x[LOW + r + sign * b * d] for b in (-1, 0, 1)]
        sums = []
        for a in range(3):
            t = [taps[l, 3 * a + b] * lines[b] for b in range(3)]
            sums.append(t[0] + t[1] + t[2])
        fwd, back = (d, LANES - d) if sign > 0 else (LANES - d, d)
        return sums[1] + pltpu.roll(sums[0], fwd, 1) + pltpu.roll(sums[2], back, 1)

    xs = [x0, x1]
    for l in range(layers):
        d = dil[l]
        x = xs[l]
        for m in range(1, HALO + 1):
            x[LOW - m] = x[LOW + m]
        base = sub_pos * HALO * (l + 1)

        def layer(i, _, l=l, d=d, x=x, base=base):
            r0 = base + i * BATCH
            hidden = []
            for j in range(BATCH):
                summed = conv(x, l, d, r0 + j, 1)
                hidden.append(jnp.maximum(summed, 0.0).astype(jnp.bfloat16))
                h[l, r0 + j] = hidden[j]
            upd = mm(spread[2 * l], jnp.concatenate(hidden, axis=0))
            upd = upd.reshape(BATCH, chans, LANES)
            for j in range(BATCH):
                new = (x[LOW + r0 + j] + upd[j]) * mask(r0 + j)
                if l + 1 < layers:
                    xs[l + 1][LOW + r0 + j] = new
                else:
                    picture[pl.ds(i * BATCH + j, 1), :] = jnp.sum(new * ro, axis=0, keepdims=True)
            return 0

        lax.fori_loop(0, (rows - HALO * (l + 1)) // BATCH, layer, 0, unroll=2)

    shown = picture[pl.ds(own_at, own_rows), :] * own_lane
    contact[...] = pltpu.roll(shown, lax.rem(LANES - turn, LANES), 1)
    for c in range(chan_count):
        rest[c] = jnp.zeros((chans, LANES), jnp.float32)

    def pull(l, r0, source, target):
        high, low = split(jnp.concatenate(source, axis=0))
        gh = mm(spread[2 * l + 1], high) + mm(spread[2 * l + 1], low)
        gh = gh.astype(jnp.bfloat16).astype(jnp.float32).reshape(BATCH, chans, LANES)
        for j in range(BATCH):
            on = h[l, r0 + j].astype(jnp.float32) > 0
            target[LOW + r0 + j] = jnp.where(on, gh[j], 0.0)

    def weight_grads(l, x, d, g_out, g_sum):
        acc[...] = jnp.zeros_like(acc)

        def body(i, sums):
            r0 = own_start + i * BATCH
            g = (g_out[pl.ds(r0, BATCH)] * own_lane).astype(jnp.bfloat16).reshape(wide, LANES)
            acc[...] += mm(h[l, pl.ds(r0, BATCH)].reshape(wide, LANES), g, NT)
            for j in range(BATCH):
                r = r0 + j
                g0 = g_sum[LOW + r] * own_lane
                moved = (pltpu.roll(g0, LANES - d, 1), g0, pltpu.roll(g0, d, 1))
                lines = [x[LOW + r + b * d] for b in (-1, 0, 1)]
                sums = tuple(sums[t] + moved[t // 3] * lines[t % 3] for t in range(9))
            return sums

        zero = jnp.zeros((chans, LANES), jnp.float32)
        sums = lax.fori_loop(0, own_rows // BATCH, body, (zero,) * 9)
        tile = jnp.zeros((chans, LANES), jnp.float32)
        for t in range(9):
            line = jnp.sum(sums[t], axis=1, keepdims=True)
            off = width + layers * chan_dev + 9 * l + t
            tile = tile + jnp.where(lane == off, line, 0.0)
        tall = jnp.sum(jnp.where(diag, acc[...], 0.0).reshape(BATCH, chans, wide), axis=0)
        row_e = lax.rem(lax.broadcasted_iota(jnp.int32, (wide, LANES), 0), chans)
        col_e = lax.broadcasted_iota(jnp.int32, (wide, LANES), 1) - width - l * chan_dev
        for c in range(chan_count):
            hit = (col_e >= 0) & (col_e < chan_dev) & (row_e == col_e + c * chan_dev)
            rest[c] = rest[c] + tile + mm(tall, hit.astype(jnp.float32), precision=EXACT)

    def last_out(i, _):
        r0 = sub_pos * 2 * HALO + i * BATCH
        lines = []
        for j in range(BATCH):
            line = cot[pl.ds(i * BATCH + j, 1), :] * mask(r0 + j)
            lines.append(ro * line)
            go[r0 + j] = lines[j]
        pull(1, r0, lines, gs)
        return 0

    lax.fori_loop(0, (rows - 2 * HALO) // BATCH, last_out, 0, unroll=3)
    weight_grads(1, x1, dil[1], go, gs)

    def fold(l, d, g, target):
        for m in range(1, HALO + 1):
            target[m] = target[m] + is_low * conv(g, l, d, -m, -1)

    def back_field(i, _):
        r0 = own_start + i * BATCH
        for j in range(BATCH):
            gf[r0 + j] = go[r0 + j] + conv(gs, 1, dil[1], r0 + j, -1)
        return 0

    lax.fori_loop(0, own_rows // BATCH, back_field, 0)
    fold(1, dil[1], gs, gf)

    def first_out(i, _):
        r0 = own_start + i * BATCH
        lines = []
        for j in range(BATCH):
            lines.append(gf[r0 + j] * (mask(r0 + j) * own_lane))
            go1[r0 + j] = lines[j]
        pull(0, r0, lines, gs1)
        return 0

    lax.fori_loop(0, own_rows // BATCH, first_out, 0, unroll=2)
    weight_grads(0, x0, dil[0], go1, gs1)

    def back_first(i, _):
        r0 = sub_pos * 2 * HALO + i * BATCH
        for j in range(BATCH):
            gf[r0 + j] = go1[r0 + j] + conv(gs1, 0, dil[0], r0 + j, -1)
        return 0

    lax.fori_loop(0, (rows - 2 * HALO) // BATCH, back_first, 0)
    fold(0, dil[0], gs1, gf)

    def to_profile(i, carry):
        near, far = carry
        r = sub_pos * 2 * HALO + i
        k = k_base + r
        g = gf[r] * mask(r)
        moved = pltpu.roll(env[...], lax.rem(2 * LANES - k, 2 * LANES), 1)[:, :LANES]
        near = near + g * moved
        part = jnp.concatenate([g * env[:, :LANES], jnp.zeros((chans, LANES), jnp.float32)], axis=1)
        far = far + pltpu.roll(part, k, 1)
        return near, far

    near, far = lax.fori_loop(
        0, rows - 2 * HALO, to_profile,
        (jnp.zeros((chans, LANES), jnp.float32), jnp.zeros((chans, 2 * LANES), jnp.float32)),
        unroll=8,
    )
    near = far[:, :LANES] + near
    whole = jnp.concatenate([near, far[:, LANES:], zero], axis=1)
    whole = pltpu.roll(whole, lead, 1)
    for b in range(gpad.shape[0]):
        gpad[b] = zero
    for b in range(3):
        gpad[tile + b] = whole[:, b * LANES : (b + 1) * LANES]

    rows_trans = tcot.shape[1]
    row_start = pl.multiple_of((chan_pos * 2 + sub_pos) * rows_trans, 8)
    for n in range(tcot.shape[0]):
        p, q = pairs[n, 0], pairs[n, 1]
        first_rows = prof[pl.ds(pl.multiple_of(p * LANES + row_start, 8), rows_trans), :] * ro_row[...]
        row_pos = p * LANES + row_start + lax.broadcasted_iota(jnp.int32, (rows_trans, LANES), 0)
        col_pos = q * LANES + lax.broadcasted_iota(jnp.int32, (rows_trans, LANES), 1)
        cross = (end_of(row_pos) != end_of(col_pos)).astype(jnp.float32)
        maps[n] = mm(first_rows, prof_t[1 + q], NN, EXACT) * cross
        spent[...] = jnp.zeros_like(spent)
        spent[pl.ds(row_start, rows_trans), :] = tcot[n] * cross
        to_first = mm(prof_t[1 + q], spent[...], NT, EXACT) * ro
        to_second = mm(prof_t[1 + p] * ro, spent[...], NN, EXACT)
        gpad[1 + p] = gpad[1 + p] + to_first
        gpad[1 + q] = gpad[1 + q] + to_second

    pieces = []
    for b in range(seq_count):
        part[b] = gpad[1 + b].astype(jnp.bfloat16)
        pieces.append(split(gpad[1 + b]))
    for c in range(chan_count):
        total_proj = jnp.zeros((chans, width), jnp.float32)
        for b in range(seq_count):
            block = feats[c, b]
            total_proj = total_proj + mm(pieces[b][0], block, NT) + mm(pieces[b][1], block, NT)
        blank = jnp.zeros((chans, LANES - width), jnp.float32)
        misc[c] = (rest[c] + jnp.concatenate([total_proj, blank], axis=1)).astype(jnp.bfloat16)


def per_device(
    features, proj, kernel, mix, readout, dilations, chrom_lengths, pairs, contact_cot, trans_cot
):
    f32, bf16 = jnp.float32, jnp.bfloat16
    bin_dev, width = features.shape
    chans = proj.shape[1]
    band_dev = contact_cot.shape[0]
    layers, chan_dev = kernel.shape[:2]
    seq_count, chan_count = lax.axis_size("seq"), lax.axis_size("chan")
    total = bin_dev * seq_count
    rows = band_dev + 3 * HALO
    smem = pl.BlockSpec(memory_space=pltpu.SMEM)
    vmem = pl.BlockSpec(memory_space=pltpu.VMEM)
    shape = jax.ShapeDtypeStruct
    proj_t = proj.T

    def sems(count):
        return [pltpu.SemaphoreType.DMA((count,))] * 2

    gathered = pl.pallas_call(
        gather_kernel,
        out_shape=(
            shape((chan_count, seq_count, width, bin_dev), bf16),
            shape((chan_count, chans, width), bf16),
            shape((chan_count, layers, chan_dev, chans), bf16),
            shape((chan_count, layers, chan_dev, 9), f32),
            shape((HALO, bin_dev), f32),
            shape((band_dev, bin_dev), f32),
            shape((HALO, bin_dev), f32),
        ),
        in_specs=[vmem] * 5,
        out_specs=(vmem,) * 7,
        scratch_shapes=[
            *sems(seq_count * chan_count - 1), *sems(3 * (chan_count - 1)), *sems(3)
        ],
        compiler_params=pltpu.CompilerParams(collective_id=0, has_side_effects=True),
    )(features.T, proj_t, mix.transpose(0, 2, 1), kernel, contact_cot)
    feats, projs, mixes, taps, edge, side, side_edge = gathered

    field = pltpu.VMEM((2 * LOW + rows, chans, LANES), f32)
    plain = pltpu.VMEM((rows, chans, LANES), f32)
    wide = BATCH * chans
    contact, maps, part, misc = pl.pallas_call(
        band_kernel,
        out_shape=(
            shape((band_dev, LANES), f32),
            shape(trans_cot.shape, f32),
            shape((seq_count, chans, LANES), bf16),
            shape((chan_count, chans, LANES), bf16),
        ),
        in_specs=[smem] * 3 + [vmem] * 11,
        out_specs=(vmem,) * 4,
        scratch_shapes=[
            pltpu.VMEM((layers, 9, chans, LANES), f32),
            pltpu.VMEM((2 * layers, wide, wide), bf16),
            pltpu.VMEM((chans, 2 * LANES), f32),
            pltpu.VMEM((total, chans), f32),
            pltpu.VMEM((seq_count + 3, chans, LANES), f32),
            field,
            field,
            pltpu.VMEM((layers, rows, chans, LANES), bf16),
            plain,
            field,
            plain,
            plain,
            field,
            pltpu.VMEM((seq_count + 3, chans, LANES), f32),
            pltpu.VMEM((wide, wide), f32),
            pltpu.VMEM((LANES, LANES), f32),
            pltpu.VMEM((band_dev + HALO, LANES), f32),
            pltpu.VMEM((band_dev + HALO, LANES), f32),
            pltpu.VMEM((chan_count, chans, LANES), f32),
            pltpu.VMEM((chans, chans), f32),
        ],
        compiler_params=pltpu.CompilerParams(vmem_limit_bytes=48 * 1024 * 1024),
    )(
        dilations, chrom_lengths, pairs, feats, projs, mixes, taps,
        readout[:, None], readout[None, :], contact_cot, edge, side, side_edge, trans_cot,
    )
    contact, grad_features, grad_proj, grad_kernel, grad_mix = pl.pallas_call(
        reduce_kernel,
        out_shape=(
            shape((band_dev, LANES), f32),
            shape((width, bin_dev), f32),
            shape((chans, width), f32),
            shape((layers, chan_dev, 9), f32),
            shape((layers, chan_dev, chans), f32),
        ),
        in_specs=[vmem] * 4,
        out_specs=(vmem,) * 5,
        scratch_shapes=[
            pltpu.VMEM((seq_count, chans, LANES), bf16),
            pltpu.VMEM((seq_count, chan_count, chans, LANES), bf16),
            pltpu.VMEM((chan_count, band_dev, LANES), f32),
            pltpu.VMEM((chan_count, 2, chans, LANES), f32),
            pltpu.VMEM((2 * chan_count, 2, chans, LANES), f32),
            pltpu.VMEM((chans, LANES), f32),
            *sems(2 * (seq_count - 1)), *sems(2 * chan_count - 1), *sems(chan_count - 1),
        ],
        compiler_params=pltpu.CompilerParams(collective_id=1, has_side_effects=True),
    )(part, misc, contact, proj_t)
    return (contact, maps, grad_features.T, grad_proj.T, grad_kernel, grad_mix.transpose(0, 2, 1))


def solution(mesh):
    in_specs = (
        P(("groups", "seq"), "chan"),
        P("chan", None),
        P(None, "chan", None),
        P(None, None, "chan"),
        P(),
        P(),
        P(),
        P(("groups", "seq"), None),
        P("sub", ("groups", "seq")),
        P(("groups", "seq"), ("chan", "sub"), None),
    )
    out_specs = (
        P("sub", ("groups", "seq")),
        P(("groups", "seq"), ("chan", "sub"), None),
        P(("groups", "seq"), "chan"),
        P(("groups", "chan"), None),
        P("groups", "chan", None),
        P("groups", None, "chan"),
    )
    return jax.shard_map(
        per_device, mesh=mesh, in_specs=in_specs, out_specs=out_specs, check_vma=False
    )
```
